256 devices in a mesh: row: 16 (over z, y_lo), col: 16 (over x, y_hi, core).
Axes of the slice: x: 4, y: 4 (y_hi: 2, y_lo: 2; y = y_hi * 2 + y_lo), z: 8, core: 2. Of those that a mesh axis runs over, the one named last changes fastest.
Arguments:
- tensor: bfloat16 [2048, 64, 2048], P('row', None, 'col'), may hold values from -6 to 6
- loss_kind: int32 [2048, 64, 2048], P('row', None, 'col'), may hold values from 0 to 1, as said below
- factor_one: float32 [2048, 512], P(('row', 'col')), may hold values from -2 to 2
- factor_two: float32 [2048, 512], P(('col', 'row')), may hold values from -2 to 2
- factor_three: float32 [64, 512], replicated, may hold values from -2 to 2
- first_one: float32 [2048, 512], P(('row', 'col')), may hold values from -0.03 to 0.03
- second_one: float32 [2048, 512], P(('row', 'col')), may hold values from 0.0005 to 0.05
- first_two: float32 [2048, 512], P(('col', 'row')), may hold values from -0.03 to 0.03
- second_two: float32 [2048, 512], P(('col', 'row')), may hold values from 0.0005 to 0.05
- first_three: float32 [64, 512], replicated, may hold values from -0.03 to 0.03
- second_three: float32 [64, 512], replicated, may hold values from 0.0005 to 0.05
Outputs:
- new_one: float32 [2048, 512], P(('row', 'col'))
- new_two: float32 [2048, 512], P(('col', 'row'))
- new_three: float32 [64, 512], replicated
The draws below stay inside these ranges and needn't reach their ends.
Inputs may be any that keep to these rules, and one draw needn't show every extreme that they name: loss_kind takes one value on each block of 128 first-mode by 128 second-mode indices (with all 64 third-mode ones), aligned to multiples of 128 and 128, and is 1 on exactly half of these blocks.
All inputs are finite; a program needn't handle non-finite values.
Results may differ from the reference program's by a relative error of at most 0.003.
Values may be sent and summed in bfloat16 or wider, within the bound.
No kernel may reach another device: no remote copies, remote signals or barrier semaphores. Data moves between devices by JAX's collectives and lax.ppermute only.
A program may use at most 128 MiB of HBM per device.

```python
import math
import jax
import jax.numpy as jnp
from jax import lax

TI = 128
TJ = 128
K = 64
R = 512
ITERS = 2
STEP = 10
I = 2048
J = 2048
N_ROW = 16


def draw_tensor(key, part):
    key_offset, key_gain, key_noise = jax.random.split(key, 3)
    row_blocks = I // TI
    col_blocks = J // TJ
    block_shape = (row_blocks, 1, 1, col_blocks, 1)
    full_shape = (row_blocks, TI, K, col_blocks, TJ)
    offset = jax.random.uniform(key_offset, block_shape, jnp.float32, -1.0, 1.0)
    gain = jnp.exp(jax.random.uniform(key_gain, block_shape, jnp.float32, -1.5, 0.7))
    noise = jax.random.normal(key_noise, full_shape, jnp.float32)
    values = jnp.clip(offset + gain * noise, -6.0, 6.0)
    return values.reshape(I, K, J).astype(jnp.bfloat16)


def draw_loss_kind(key, part):
    row_blocks = I // TI
    col_blocks = J // TJ
    order = jax.random.permutation(key, row_blocks * col_blocks)
    block_kind = (order % 2).astype(jnp.int32).reshape(row_blocks, 1, 1, col_blocks, 1)
    return jnp.broadcast_to(block_kind, (row_blocks, TI, K, col_blocks, TJ)).reshape(I, K, J)


def shard_levels(key, shape, pieces, smallest, high):
    factor_of = 1.0
    for dim, blocks in pieces:
        heights = jax.random.uniform(jax.random.fold_in(jax.random.fold_in(key, 6), dim), (blocks,), jnp.float32, smallest / len(pieces), high / len(pieces))
        factor_of = factor_of * jnp.repeat(jnp.exp(heights), shape[dim] // blocks).reshape((-1,) + (1,) * (len(shape) - 1 - dim))
    return factor_of


def bell_draw(rng, dims, deviation, most, cuts=(), held_as=jnp.bfloat16):
    level = shard_levels(rng, dims, cuts, -0.22, 0.18) if cuts else 1.0
    drawn = jax.random.normal(rng, dims, jnp.float32) * deviation * level
    return jnp.minimum(jnp.maximum(drawn, -most), most).astype(held_as)


def setup_inputs(seed: int = 0) -> dict:
    seeds = jax.random.split(jax.random.key(seed), 12)
    tensor = draw_tensor(jax.random.fold_in(seeds[11], 71), 0)
    loss_kind = draw_loss_kind(jax.random.fold_in(seeds[11], 71), 0)
    factor_one = bell_draw(seeds[2], (I, R), 0.35, 2.0, ((0, 256),), jnp.float32)
    factor_two = bell_draw(seeds[3], (J, R), 0.35, 2.0, ((0, 256),), jnp.float32)
    factor_three = bell_draw(seeds[4], (K, R), 0.35, 2.0, (), jnp.float32)
    first_one = bell_draw(seeds[5], (I, R), 0.005, 0.03, ((0, 256),), jnp.float32)
    second_one = jnp.clip(jnp.exp(math.log(0.05) - 4.6051702 * jax.random.uniform(seeds[6], (I, R), jnp.float32) ** shard_levels(seeds[6], (I, R), ((0, 256),), -0.2, 0.2)), 0.0005, 0.05)
    first_two = bell_draw(seeds[7], (J, R), 0.005, 0.03, ((0, 256),), jnp.float32)
    second_two = jnp.clip(jnp.exp(math.log(0.05) - 4.6051702 * jax.random.uniform(seeds[8], (J, R), jnp.float32) ** shard_levels(seeds[8], (J, R), ((0, 256),), -0.2, 0.2)), 0.0005, 0.05)
    first_three = bell_draw(seeds[9], (K, R), 0.005, 0.03, (), jnp.float32)
    second_three = jnp.clip(jnp.exp(jax.random.uniform(seeds[10], (K, R), jnp.float32, math.log(0.0005), math.log(0.05))), 0.0005, 0.05)
    return dict(tensor=tensor, loss_kind=loss_kind, factor_one=factor_one, factor_two=factor_two, factor_three=factor_three, first_one=first_one, second_one=second_one, first_two=first_two, second_two=second_two, first_three=first_three, second_three=second_three)


learn_rate = 0.05
beta_one = 0.8
beta_two = 0.95
adam_eps = 1e-08

def loss_slope(rebuilt, values, kinds):
    excess = rebuilt - values
    huber_part = jnp.clip(excess, -1.0, 1.0)
    target = jnp.where(values > 0, 1.0, 0.0).astype(rebuilt.dtype)
    logit_part = jax.nn.sigmoid(rebuilt) - target
    return jnp.where(kinds == 1, logit_part, huber_part)

def adam_step(param, first, second, grad, counter):
    first = beta_one * first + (1.0 - beta_one) * grad
    second = beta_two * second + (1.0 - beta_two) * grad * grad
    corr_one = 1.0 - beta_one ** counter
    corr_two = 1.0 - beta_two ** counter
    param = param - learn_rate * (first / corr_one) / (jnp.sqrt(second / corr_two) + adam_eps)
    return (param, first, second)

def all_grads(tensor, loss_kind, half_one, half_two, half_three):
    three_f = half_three.astype(jnp.float32)
    blocks = (tensor.reshape(N_ROW, TI, K, J), loss_kind.reshape(N_ROW, TI, K, J), half_one.reshape(N_ROW, TI, R))

    def block_step(carry, items):
        grad_two, grad_three = carry
        data_blk, kind_blk, one_blk = items
        one_f = one_blk.astype(jnp.float32)
        scaled_rows = (one_f[:, None, :] * three_f[None, :, :]).astype(jnp.bfloat16).reshape(TI * K, R)
        rebuilt = lax.dot_general(scaled_rows, half_two, (((1,), (1,)), ((), ())), preferred_element_type=jnp.float32)
        values = data_blk.reshape(TI * K, J).astype(jnp.float32)
        deriv_bf = loss_slope(rebuilt, values, kind_blk.reshape(TI * K, J)).astype(jnp.bfloat16)
        projected = jnp.dot(deriv_bf, half_two, preferred_element_type=jnp.float32).reshape(TI, K, R)
        grad_one = lax.optimization_barrier(jnp.sum(projected * three_f[None, :, :], axis=1))
        grad_three = grad_three + lax.optimization_barrier(jnp.sum(projected * one_f[:, None, :], axis=0))
        grad_two = grad_two + lax.dot_general(deriv_bf, scaled_rows, (((0,), (0,)), ((), ())), preferred_element_type=jnp.float32)
        return ((grad_two, grad_three), grad_one)
    start = (jnp.zeros((J, R), jnp.float32), jnp.zeros((K, R), jnp.float32))
    (grad_two, grad_three), grad_one = lax.scan(block_step, start, blocks)
    grad_one = grad_one.reshape(I, R) / math.sqrt(J * K)
    grad_two = grad_two / math.sqrt(I * K)
    grad_three = grad_three / math.sqrt(I * J)
    return (grad_one, grad_two, grad_three)

def reference(tensor, loss_kind, factor_one, factor_two, factor_three, first_one, second_one, first_two, second_two, first_three, second_three):
    start_one, start_two, start_three = (factor_one, factor_two, factor_three)
    for iteration in range(ITERS):
        grad_one, grad_two, grad_three = all_grads(tensor, loss_kind, factor_one.astype(jnp.bfloat16), factor_two.astype(jnp.bfloat16), factor_three.astype(jnp.bfloat16))
        counter = STEP + iteration + 1
        factor_one, first_one, second_one = adam_step(factor_one, first_one, second_one, grad_one, counter)
        factor_two, first_two, second_two = adam_step(factor_two, first_two, second_two, grad_two, counter)
        factor_three, first_three, second_three = adam_step(factor_three, first_three, second_three, grad_three, counter)
    spread = learn_rate * ITERS
    return ((start_one - factor_one) / spread, (start_two - factor_two) / spread, (start_three - factor_three) / spread)
```

```python
import functools
import math

import jax
import jax.numpy as jnp
from jax import lax
from jax.experimental import pallas as pl
from jax.experimental.pallas import tpu as pltpu
from jax.sharding import PartitionSpec as P

ITERS = 2
STEP = 10
BLOCK = 8

learn_rate = 0.05
beta_one = 0.8
beta_two = 0.95
adam_eps = 1e-08

f32 = jnp.float32
bf16 = jnp.bfloat16


def adam_step(param, first, second, grad, counter):
    first = beta_one * first + (1.0 - beta_one) * grad
    second = beta_two * second + (1.0 - beta_two) * grad * grad
    corr_one = 1.0 - beta_one**counter
    corr_two = 1.0 - beta_two**counter
    param = param - learn_rate * (first / corr_one) / (jnp.sqrt(second / corr_two) + adam_eps)
    return (param, first, second)


def grads_kernel(scales, kind_ref, data_ref, one_ref, two_ref, three_ref, ga_ref, gb_ref, gc_ref, acc_b, acc_c):
    step = pl.program_id(0)
    depth, rank = three_ref.shape
    cols = two_ref.shape[0]

    @pl.when(step == 0)
    def _():
        acc_b[...] = jnp.zeros_like(acc_b)
        acc_c[...] = jnp.zeros_like(acc_c)

    one_f = one_ref[...].astype(f32)
    three_f = three_ref[...].astype(f32)
    two = two_ref[...]
    scaled = (one_f[:, None, :] * three_f[None, :, :]).astype(bf16).reshape(BLOCK * depth, rank)
    rebuilt = lax.dot_general(scaled, two, (((1,), (1,)), ((), ())), preferred_element_type=f32)
    values = data_ref[...].reshape(BLOCK * depth, cols).astype(f32)

    def finish(deriv):
        deriv = deriv.astype(bf16)
        proj = jnp.dot(deriv, two, preferred_element_type=f32).reshape(BLOCK, depth, rank)
        ga_ref[...] = (jnp.sum(proj * three_f[None], axis=1) * scales[0]).astype(ga_ref.dtype)
        acc_c[...] += jnp.sum(proj * one_f[:, None, :], axis=0)
        acc_b[...] += lax.dot_general(
            deriv, scaled, (((0,), (0,)), ((), ())), preferred_element_type=f32
        )

    logit = 0.5 * jnp.tanh(0.5 * rebuilt) + jnp.where(values > 0, -0.5, 0.5)
    huber = jnp.clip(rebuilt - values, -1.0, 1.0)
    finish(jnp.where(kind_ref[0] == 1, logit, huber))

    @pl.when(step == pl.num_programs(0) - 1)
    def _():
        gb_ref[...] = (acc_b[...] * scales[1]).astype(gb_ref.dtype)
        gc_ref[...] = (acc_c[...] * scales[2]).astype(gc_ref.dtype)


def tile_grads(kind, tensor, half_one, half_two, half_three, scales):
    rows, depth, cols = tensor.shape
    rank = half_one.shape[1]
    whole = lambda shape: pl.BlockSpec(shape, lambda i: (0,) * len(shape))
    return pl.pallas_call(
        functools.partial(grads_kernel, scales),
        grid=(rows // BLOCK,),
        in_specs=[
            pl.BlockSpec(memory_space=pltpu.SMEM),
            pl.BlockSpec((BLOCK, depth, cols), lambda i: (i, 0, 0)),
            pl.BlockSpec((BLOCK, rank), lambda i: (i, 0)),
            whole((cols, rank)),
            whole((depth, rank)),
        ],
        out_specs=[
            pl.BlockSpec((BLOCK, rank), lambda i: (i, 0)),
            whole((cols, rank)),
            whole((depth, rank)),
        ],
        out_shape=[
            jax.ShapeDtypeStruct((rows, rank), f32),
            jax.ShapeDtypeStruct((cols, rank), bf16),
            jax.ShapeDtypeStruct((depth, rank), bf16),
        ],
        scratch_shapes=[pltpu.VMEM((cols, rank), f32), pltpu.VMEM((depth, rank), f32)],
        compiler_params=pltpu.CompilerParams(vmem_limit_bytes=32 << 20),
        cost_estimate=pl.CostEstimate(
            flops=6 * rows * depth * cols * rank, bytes_accessed=4 << 20, transcendentals=rows * depth * cols
        ),
    )(kind, tensor, half_one, half_two, half_three)


def spread_out(part, axis):
    size = lax.axis_size(axis)
    return lax.all_to_all(jnp.broadcast_to(part[None], (size,) + part.shape), axis, 0, 0)


def swap_sum(parts, axis):
    return jnp.sum(lax.all_to_all(parts, axis, 0, 0).astype(f32), axis=0)


def shards(
    tensor, loss_kind, factor_one, factor_two, factor_three,
    first_one, second_one, first_two, second_two, first_three, second_three,
):
    tile_rows, tile_depth, tile_cols = tensor.shape
    n_row, n_col = lax.axis_size("row"), lax.axis_size("col")
    rank = factor_one.shape[1]
    own = factor_one.shape[0]
    own_two = factor_two.shape[0]
    own_three = tile_depth // n_col
    full_rows, full_cols = tile_rows * n_row, tile_cols * n_col
    scales = (
        1.0 / math.sqrt(full_cols * tile_depth),
        1.0 / math.sqrt(full_rows * tile_depth),
        1.0 / math.sqrt(full_rows * full_cols),
    )
    kind = loss_kind[0, 0, :1]
    place = lax.axis_index("col") * own_three
    mine = lambda x: lax.dynamic_slice_in_dim(x, place, own_three, 0)
    half_three = factor_three.astype(bf16)
    part_three, first_three, second_three = mine(factor_three), mine(first_three), mine(second_three)
    start_one, start_two, start_three = (factor_one, factor_two, part_three)
    half_one = spread_out(factor_one.astype(bf16), "col").reshape(tile_rows, rank)
    half_two = spread_out(factor_two.astype(bf16), "row").reshape(tile_cols, rank)
    for iteration in range(ITERS):
        grad_one, grad_two, grad_three = tile_grads(kind, tensor, half_one, half_two, half_three, scales)
        sent = jnp.concatenate(
            [grad_one.astype(bf16).reshape(n_col, own, rank), grad_three.reshape(n_col, own_three, rank)], axis=1
        )
        got = swap_sum(sent, "col")
        grad_one, grad_three = got[:own], got[own:]
        sent = jnp.concatenate(
            [
                grad_two.reshape(n_row, own_two, rank),
                jnp.broadcast_to(grad_three.astype(bf16)[None], (n_row, own_three, rank)),
            ],
            axis=1,
        )
        got = swap_sum(sent, "row")
        grad_two, grad_three = got[:own_two], got[own_two:]
        counter = STEP + iteration + 1
        factor_one, first_one, second_one = adam_step(factor_one, first_one, second_one, grad_one, counter)
        factor_two, first_two, second_two = adam_step(factor_two, first_two, second_two, grad_two, counter)
        part_three, first_three, second_three = adam_step(
            part_three, first_three, second_three, grad_three, counter
        )
        if iteration < ITERS - 1:
            halves = spread_out(jnp.concatenate([factor_one, part_three]).astype(bf16), "col")
            half_one = halves[:, :own].reshape(tile_rows, rank)
            half_three = halves[:, own:].reshape(tile_depth, rank)
            half_two = spread_out(factor_two.astype(bf16), "row").reshape(tile_cols, rank)
    spread = learn_rate * ITERS
    new_three = spread_out((start_three - part_three) / spread, "col").reshape(tile_depth, rank)
    return ((start_one - factor_one) / spread, (start_two - factor_two) / spread, new_three)


def solution(mesh):
    in_specs = (
        P("row", None, "col"),
        P("row", None, "col"),
        P(("row", "col"), None),
        P(("col", "row"), None),
        P(),
        P(("row", "col"), None),
        P(("row", "col"), None),
        P(("col", "row"), None),
        P(("col", "row"), None),
        P(),
        P(),
    )
    out_specs = (P(("row", "col"), None), P(("col", "row"), None), P())
    return jax.shard_map(shards, mesh=mesh, in_specs=in_specs, out_specs=out_specs, check_vma=False)
```

```python
import functools
import math

import jax
import jax.numpy as jnp
from jax import lax
from jax.experimental import pallas as pl
from jax.experimental.pallas import tpu as pltpu
from jax.sharding import PartitionSpec as P

ITERS = 2
STEP = 10
BLOCK = 64
SUB = 4

learn_rate = 0.05
beta_one = 0.8
beta_two = 0.95
adam_eps = 1e-08

f32 = jnp.float32
bf16 = jnp.bfloat16

CORE, Y_HI, X_ONE = 1, 2, 4


def adam_step(param, first, second, grad, counter):
    first = beta_one * first + (1.0 - beta_one) * grad
    second = beta_two * second + (1.0 - beta_two) * grad * grad
    corr_one = 1.0 - beta_one**counter
    corr_two = 1.0 - beta_two**counter
    param = param - learn_rate * (first / corr_one) / (jnp.sqrt(second / corr_two) + adam_eps)
    return (param, first, second)


def piece_codes():
    return [y + x for y in (0, Y_HI) for x in (0, X_ONE, 2 * X_ONE, 3 * X_ONE)]


def slope_kernel(scales, with_three, ids_ref, data_ref, near_ref, far_ref, two_ref, three_ref,
                 sent_ref, slope_ref, one_ref, three_out_ref, ga_acc, gc_acc):
    step = pl.program_id(0)
    n_slab, own, rank = one_ref.shape
    depth = three_out_ref.shape[0] * three_out_ref.shape[1]
    cols = two_ref.shape[0]

    @pl.when(step == 0)
    def _():
        here = ids_ref[1]
        for place, code in enumerate(piece_codes()):
            slab = here ^ code
            one_ref[slab] = near_ref[place][:own]
            one_ref[slab ^ CORE] = far_ref[place][:own]
            if with_three:
                three_out_ref[slab // 2] = near_ref[place][own:]
        if not with_three:
            three_out_ref[...] = three_ref[...]
        gc_acc[...] = jnp.zeros_like(gc_acc)

    def run(logistic):
        two = two_ref[...]
        three = three_out_ref[...].reshape(depth, rank)
        three_f = three.astype(f32)
        slabs = BLOCK // own
        one = one_ref[pl.ds(step * slabs, slabs)].reshape(BLOCK, rank)
        n = BLOCK // SUB

        def rows(s):
            return slice(s * SUB, (s + 1) * SUB)

        def rebuild(s):
            scaled = (one[rows(s)][:, None, :] * three[None]).reshape(SUB * depth, rank)
            return lax.dot_general(scaled, two, (((1,), (1,)), ((), ())), preferred_element_type=f32)

        def slope(s, rebuilt):
            values = data_ref[rows(s)].reshape(SUB * depth, cols).astype(f32)
            if logistic:
                out = 0.5 * jnp.tanh(0.5 * rebuilt) + jnp.where(values > 0, -0.5, 0.5)
            else:
                out = jnp.clip(rebuilt - values, -1.0, 1.0)
            out = out.astype(bf16)
            slope_ref[rows(s)] = out.reshape(SUB, depth, cols)
            return out

        def project(deriv):
            return jnp.dot(deriv, two, preferred_element_type=f32).reshape(SUB, depth, rank)

        rebuilt, derivs, projs = {}, {}, {}
        grad_one, grad_three = [], None
        for t in range(n + 3):
            if t < n:
                rebuilt[t] = rebuild(t)
            if 0 <= t - 1 < n:
                derivs[t - 1] = slope(t - 1, rebuilt.pop(t - 1))
            if 0 <= t - 2 < n:
                projs[t - 2] = project(derivs.pop(t - 2))
            if 0 <= t - 3 < n:
                proj = projs.pop(t - 3)
                one_f = one[rows(t - 3)].astype(f32)
                grad_one.append(jnp.sum(proj * three_f[None], axis=1))
                part = jnp.sum(proj * one_f[:, None, :], axis=0)
                grad_three = part if grad_three is None else grad_three + part
        ga_acc[pl.ds(step * BLOCK, BLOCK)] = jnp.concatenate(grad_one)
        gc_acc[...] += grad_three

    pl.when(ids_ref[0] == 1)(lambda: run(True))
    pl.when(ids_ref[0] != 1)(lambda: run(False))

    @pl.when(step == pl.num_programs(0) - 1)
    def _():
        deep = three_out_ref.shape[1]
        for slab in range(n_slab):
            low = slab // 2 * deep
            sent_ref[slab] = jnp.concatenate(
                [ga_acc[slab * own:(slab + 1) * own] * scales[0], gc_acc[low:low + deep] * scales[2]]
            ).astype(bf16)


def slopes(ids, tensor, near, far, half_two, half_three, scales, with_three):
    rows, depth, cols = tensor.shape
    rank = half_two.shape[1]
    slabs, own = 2 * near.shape[0], rows // (2 * near.shape[0])
    deep = 2 * depth // slabs
    whole = lambda shape: pl.BlockSpec(shape, lambda i: (0,) * len(shape))
    return pl.pallas_call(
        functools.partial(slope_kernel, scales, with_three),
        grid=(rows // BLOCK,),
        in_specs=[
            pl.BlockSpec(memory_space=pltpu.SMEM),
            pl.BlockSpec((BLOCK, depth, cols), lambda i: (i, 0, 0)),
            whole(near.shape),
            whole(far.shape),
            whole((cols, rank)),
            whole(half_three.shape),
        ],
        out_specs=[
            whole((slabs, own + deep, rank)),
            pl.BlockSpec((BLOCK, depth, cols), lambda i: (i, 0, 0)),
            whole((slabs, own, rank)),
            whole((slabs // 2, deep, rank)),
        ],
        out_shape=[
            jax.ShapeDtypeStruct((slabs, own + deep, rank), bf16),
            jax.ShapeDtypeStruct((rows, depth, cols), bf16),
            jax.ShapeDtypeStruct((slabs, own, rank), bf16),
            jax.ShapeDtypeStruct((slabs // 2, deep, rank), bf16),
        ],
        scratch_shapes=[pltpu.VMEM((rows, rank), f32), pltpu.VMEM((depth, rank), f32)],
        compiler_params=pltpu.CompilerParams(vmem_limit_bytes=48 << 20),
        cost_estimate=pl.CostEstimate(
            flops=8 * rows * depth * cols * rank, bytes_accessed=4 << 20, transcendentals=rows * depth * cols
        ),
    )(ids, tensor, near, far, half_two, half_three)


def second_kernel(scale, slope_ref, one_ref, three_ref, out_ref, acc):
    step = pl.program_id(0)
    block, depth, cols = slope_ref.shape
    rank = one_ref.shape[2]
    one = one_ref[...].reshape(block, rank)
    three = three_ref[...].reshape(depth, rank)
    scaled = (one[:, None, :] * three[None]).reshape(block * depth, rank)
    part = lax.dot_general(
        slope_ref[...].reshape(block * depth, cols), scaled, (((0,), (0,)), ((), ())), preferred_element_type=f32
    )

    @pl.when(step == 0)
    def _():
        acc[...] = part

    @pl.when(step != 0)
    def _():
        acc[...] += part

    @pl.when(step == pl.num_programs(0) - 1)
    def _():
        out_ref[...] = (acc[...] * scale).astype(bf16)


def second_grad(slope, ones, threes, scale):
    rows, depth, cols = slope.shape
    slabs, own, rank = ones.shape
    block = 32
    return pl.pallas_call(
        functools.partial(second_kernel, scale),
        grid=(rows // block,),
        in_specs=[
            pl.BlockSpec((block, depth, cols), lambda i: (i, 0, 0)),
            pl.BlockSpec((block // own, own, rank), lambda i: (i, 0, 0)),
            pl.BlockSpec(threes.shape, lambda i: (0, 0, 0)),
        ],
        out_specs=pl.BlockSpec((cols, rank), lambda i: (0, 0)),
        out_shape=jax.ShapeDtypeStruct((cols, rank), bf16),
        scratch_shapes=[pltpu.VMEM((cols, rank), f32)],
        compiler_params=pltpu.CompilerParams(vmem_limit_bytes=32 << 20),
        cost_estimate=pl.CostEstimate(
            flops=4 * rows * depth * cols * rank, bytes_accessed=2 << 20, transcendentals=0
        ),
    )(slope, ones, threes)


def spread_out(part, axis, groups=None):
    size = lax.axis_size(axis) if groups is None else len(groups[0])
    whole = jnp.broadcast_to(part[None], (size,) + part.shape)
    return lax.all_to_all(whole, axis, 0, 0, axis_index_groups=groups)


def swap_sum(parts, axis):
    return jnp.sum(lax.all_to_all(parts, axis, 0, 0).astype(f32), axis=0)


def swap(part, code):
    size = lax.axis_size("col")
    return lax.ppermute(part, "col", [(i, i ^ code) for i in range(size)])


def gather_col(part):
    pieces = [part] + [swap(part, m * X_ONE) for m in (1, 2, 3)]
    half = jnp.stack(pieces)
    near = jnp.concatenate([half, swap(half, Y_HI)])
    return near, swap(near, CORE)


def shards(
    tensor, loss_kind, factor_one, factor_two, factor_three,
    first_one, second_one, first_two, second_two, first_three, second_three,
):
    tile_rows, tile_depth, tile_cols = tensor.shape
    n_row, n_col = lax.axis_size("row"), lax.axis_size("col")
    rank = factor_one.shape[1]
    own, own_two = factor_one.shape[0], factor_two.shape[0]
    deep = 2 * tile_depth // n_col
    full_rows, full_cols = tile_rows * n_row, tile_cols * n_col
    scales = (
        1.0 / math.sqrt(full_cols * tile_depth),
        1.0 / math.sqrt(full_rows * tile_depth),
        1.0 / math.sqrt(full_rows * full_cols),
    )
    here = lax.axis_index("col")
    ids = jnp.stack([loss_kind[0, 0, 0], here.astype(jnp.int32)])
    mine = lambda x: lax.dynamic_slice_in_dim(x, here // 2 * deep, deep, 0)
    half_three = factor_three.astype(bf16).reshape(n_col // 2, deep, rank)
    part_three, first_three, second_three = mine(factor_three), mine(first_three), mine(second_three)
    start_one, start_two, start_three = (factor_one, factor_two, part_three)
    half_two = spread_out(factor_two.astype(bf16), "row").reshape(tile_cols, rank)
    near, far = gather_col(factor_one.astype(bf16))
    for iteration in range(ITERS):
        sent, slope, ones, threes = slopes(
            ids, tensor, near, far, half_two, half_three, scales, iteration > 0
        )
        grad_two = second_grad(slope, ones, threes, scales[1])
        got = swap_sum(sent, "col")
        grad_one, grad_three = got[:own], got[own:]
        sent = jnp.concatenate(
            [
                grad_two.reshape(n_row, own_two, rank),
                jnp.broadcast_to(grad_three.astype(bf16)[None], (n_row, deep, rank)),
            ],
            axis=1,
        )
        got = swap_sum(sent, "row")
        grad_two, grad_three = got[:own_two], got[own_two:]
        counter = STEP + iteration + 1
        factor_one, first_one, second_one = adam_step(factor_one, first_one, second_one, grad_one, counter)
        factor_two, first_two, second_two = adam_step(factor_two, first_two, second_two, grad_two, counter)
        part_three, first_three, second_three = adam_step(
            part_three, first_three, second_three, grad_three, counter
        )
        if iteration < ITERS - 1:
            half_two = spread_out(factor_two.astype(bf16), "row").reshape(tile_cols, rank)
            near, far = gather_col(jnp.concatenate([factor_one, part_three]).astype(bf16))
            half_three = threes
    spread = learn_rate * ITERS
    chips = [[c for c in range(core, n_col, 2)] for core in range(2)]
    new_three = spread_out((start_three - part_three) / spread, "col", chips).reshape(tile_depth, rank)
    return ((start_one - factor_one) / spread, (start_two - factor_two) / spread, new_three)


def solution(mesh):
    in_specs = (
        P("row", None, "col"),
        P("row", None, "col"),
        P(("row", "col"), None),
        P(("col", "row"), None),
        P(),
        P(("row", "col"), None),
        P(("row", "col"), None),
        P(("col", "row"), None),
        P(("col", "row"), None),
        P(),
        P(),
    )
    out_specs = (P(("row", "col"), None), P(("col", "row"), None), P())
    return jax.shard_map(shards, mesh=mesh, in_specs=in_specs, out_specs=out_specs, check_vma=False)
```

```python
import functools
import math

import jax
import jax.numpy as jnp
from jax import lax
from jax.experimental import pallas as pl
from jax.experimental.pallas import tpu as pltpu
from jax.sharding import PartitionSpec as P

ITERS = 2
STEP = 10
BLOCK = 64
SUB = 4
VMEM_LIMIT = 53 << 20

learn_rate = 0.05
beta_one = 0.8
beta_two = 0.95
adam_eps = 1e-08

f32 = jnp.float32
bf16 = jnp.bfloat16

CORE, Y_HI, X_ONE = 1, 2, 4


def adam_step(param, first, second, grad, counter):
    first = beta_one * first + (1.0 - beta_one) * grad
    second = beta_two * second + (1.0 - beta_two) * grad * grad
    corr_one = 1.0 - beta_one**counter
    corr_two = 1.0 - beta_two**counter
    param = param - learn_rate * (first / corr_one) / (jnp.sqrt(second / corr_two) + adam_eps)
    return (param, first, second)


def gather_codes():
    return [y + x * X_ONE for y in (0, Y_HI) for x in range(4)]


def third_slab(col):
    return col // X_ONE * 2 + col % 2


def slope_kernel(scales, stepped, ids_ref, data_ref, near_ref, far_ref, two_in_ref, *refs):
    if stepped:
        near_three_ref, far_three_ref, *refs = refs
    else:
        three_in_ref, *refs = refs
    (sent_ref, kept_ref, slope_ref, one_ref, three_ref, two_ref, ga_acc, gc_acc) = refs
    step = pl.program_id(0)
    n_slab, own, rank = one_ref.shape
    depth = three_ref.shape[0] * three_ref.shape[1]
    cols = two_ref.shape[0] * two_ref.shape[1]
    here = ids_ref[1]

    @pl.when(step == 0)
    def _():
        for place, code in enumerate(gather_codes()):
            one_ref[here ^ code] = near_ref[place]
            one_ref[here ^ code ^ CORE] = far_ref[place]
        if stepped:
            for m in range(4):
                col = here ^ (m * X_ONE)
                three_ref[third_slab(col)] = near_three_ref[m]
                three_ref[third_slab(col ^ CORE)] = far_three_ref[m]
        else:
            three_ref[...] = three_in_ref[...]
        for slab in range(two_ref.shape[0]):
            two_ref[slab] = two_in_ref[slab][:two_ref.shape[1]]
        gc_acc[...] = jnp.zeros_like(gc_acc)

    def run(logistic):
        two = two_ref[...].reshape(cols, rank)
        three = three_ref[...].reshape(depth, rank)
        three_f = three.astype(f32)
        slabs = BLOCK // own
        one = one_ref[pl.ds(step * slabs, slabs)].reshape(BLOCK, rank)
        n = BLOCK // SUB

        def rows(s):
            return slice(s * SUB, (s + 1) * SUB)

        def rebuild(s):
            scaled = (one[rows(s)][:, None, :] * three[None]).reshape(SUB * depth, rank)
            return lax.dot_general(scaled, two, (((1,), (1,)), ((), ())), preferred_element_type=f32)

        def slope(s, rebuilt):
            values = data_ref[rows(s)].reshape(SUB * depth, cols).astype(f32)
            if logistic:
                out = 0.5 * jnp.tanh(0.5 * rebuilt) + jnp.where(values > 0, -0.5, 0.5)
            else:
                out = jnp.clip(rebuilt - values, -1.0, 1.0)
            out = out.astype(bf16)
            slope_ref[rows(s)] = out.reshape(SUB, depth, cols)
            return out

        def project(deriv):
            return jnp.dot(deriv, two, preferred_element_type=f32).reshape(SUB, depth, rank)

        rebuilt, derivs, projs = {}, {}, {}
        grad_one, grad_three = [], None
        for t in range(n + 3):
            if t < n:
                rebuilt[t] = rebuild(t)
            if 0 <= t - 1 < n:
                derivs[t - 1] = slope(t - 1, rebuilt.pop(t - 1))
            if 0 <= t - 2 < n:
                projs[t - 2] = project(derivs.pop(t - 2))
            if 0 <= t - 3 < n:
                proj = projs.pop(t - 3)
                one_f = one[rows(t - 3)].astype(f32)
                grad_one.append(jnp.sum(proj * three_f[None], axis=1))
                part = jnp.sum(proj * one_f[:, None, :], axis=0)
                grad_three = part if grad_three is None else grad_three + part
        ga_acc[pl.ds(step * slabs, slabs)] = jnp.concatenate(grad_one).reshape(slabs, own, rank)
        gc_acc[...] += grad_three.reshape(gc_acc.shape)

    pl.when(ids_ref[0] == 1)(lambda: run(True))
    pl.when(ids_ref[0] != 1)(lambda: run(False))

    @pl.when(step == pl.num_programs(0) - 1)
    def _():
        for side, out_ref in ((here, kept_ref), (here ^ CORE, sent_ref)):
            for m in range(4):
                col = side ^ (m * X_ONE)
                out_ref[m] = (ga_acc[col] * scales[0]).astype(bf16)
                out_ref[4 + m] = (gc_acc[third_slab(col)] * scales[2]).astype(bf16)
                out_ref[8 + m] = (ga_acc[col ^ Y_HI] * scales[0]).astype(bf16)


def slopes(ids, tensor, near, far, twos, threes, scales):
    rows, depth, cols = tensor.shape
    own, rank = near.shape[1:]
    slabs = rows // own
    own_two = cols // twos.shape[0]
    own_three = threes[0].shape[1]
    whole = lambda shape: pl.BlockSpec(shape, lambda i: (0,) * len(shape))
    swapped = (12, own, rank)
    return pl.pallas_call(
        functools.partial(slope_kernel, scales, len(threes) == 2),
        grid=(rows // BLOCK,),
        in_specs=[
            pl.BlockSpec(memory_space=pltpu.SMEM),
            pl.BlockSpec((BLOCK, depth, cols), lambda i: (i, 0, 0)),
            whole(near.shape),
            whole(far.shape),
            whole(twos.shape),
            *[whole(x.shape) for x in threes],
        ],
        out_specs=[
            whole(swapped),
            whole(swapped),
            pl.BlockSpec((BLOCK, depth, cols), lambda i: (i, 0, 0)),
            whole((slabs, own, rank)),
            whole((depth // own_three, own_three, rank)),
        ],
        out_shape=[
            jax.ShapeDtypeStruct(swapped, bf16),
            jax.ShapeDtypeStruct(swapped, bf16),
            jax.ShapeDtypeStruct((rows, depth, cols), bf16),
            jax.ShapeDtypeStruct((slabs, own, rank), bf16),
            jax.ShapeDtypeStruct((depth // own_three, own_three, rank), bf16),
        ],
        scratch_shapes=[
            pltpu.VMEM((twos.shape[0], own_two, rank), bf16),
            pltpu.VMEM((slabs, own, rank), f32),
            pltpu.VMEM((depth // own_three, own_three, rank), f32),
        ],
        compiler_params=pltpu.CompilerParams(vmem_limit_bytes=VMEM_LIMIT),
        cost_estimate=pl.CostEstimate(
            flops=8 * rows * depth * cols * rank, bytes_accessed=4 << 20, transcendentals=rows * depth * cols
        ),
    )(ids, tensor, near, far, twos, *threes)


def second_kernel(scale, slope_ref, one_ref, three_ref, out_ref, acc):
    step = pl.program_id(0)
    block, depth, cols = slope_ref.shape
    rank = one_ref.shape[2]
    one = one_ref[...].reshape(block, rank)
    three = three_ref[...].reshape(depth, rank)
    scaled = (one[:, None, :] * three[None]).reshape(block * depth, rank)
    part = lax.dot_general(
        slope_ref[...].reshape(block * depth, cols), scaled, (((0,), (0,)), ((), ())), preferred_element_type=f32
    )

    @pl.when(step == 0)
    def _():
        acc[...] = part

    @pl.when(step != 0)
    def _():
        acc[...] += part

    @pl.when(step == pl.num_programs(0) - 1)
    def _():
        out_ref[...] = (acc[...] * scale).astype(bf16)


def second_grad(slope, ones, threes, scale):
    rows, depth, cols = slope.shape
    slabs, own, rank = ones.shape
    block = 32
    return pl.pallas_call(
        functools.partial(second_kernel, scale),
        grid=(rows // block,),
        in_specs=[
            pl.BlockSpec((block, depth, cols), lambda i: (i, 0, 0)),
            pl.BlockSpec((block // own, own, rank), lambda i: (i, 0, 0)),
            pl.BlockSpec(threes.shape, lambda i: (0, 0, 0)),
        ],
        out_specs=pl.BlockSpec((cols, rank), lambda i: (0, 0)),
        out_shape=jax.ShapeDtypeStruct((cols, rank), bf16),
        scratch_shapes=[pltpu.VMEM((cols, rank), f32)],
        compiler_params=pltpu.CompilerParams(vmem_limit_bytes=VMEM_LIMIT),
        cost_estimate=pl.CostEstimate(
            flops=4 * rows * depth * cols * rank, bytes_accessed=2 << 20, transcendentals=0
        ),
    )(slope, ones, threes)


def place_kernel(ids_ref, near_ref, far_ref, out_ref):
    for m in range(4):
        col = ids_ref[1] ^ (m * X_ONE)
        out_ref[third_slab(col)] = near_ref[m]
        out_ref[third_slab(col ^ CORE)] = far_ref[m]


def place_third(ids, near, far):
    slabs, own, rank = near.shape
    return pl.pallas_call(
        place_kernel,
        in_specs=[pl.BlockSpec(memory_space=pltpu.SMEM)] + [pl.BlockSpec(memory_space=pltpu.VMEM)] * 2,
        out_specs=pl.BlockSpec(memory_space=pltpu.VMEM),
        out_shape=jax.ShapeDtypeStruct((2 * slabs, own, rank), near.dtype),
        compiler_params=pltpu.CompilerParams(vmem_limit_bytes=8 << 20),
    )(ids, near, far)


def swap_all(parts, axis):
    return lax.all_to_all(parts, axis, 0, 0)


def to_all(part, size):
    return jnp.broadcast_to(part[None], (size,) + part.shape)


def total(parts):
    return jnp.sum(parts.astype(f32), axis=0)


def swap(part, code):
    size = lax.axis_size("col")
    return lax.ppermute(part, "col", [(i, i ^ code) for i in range(size)])


def plus(left, right):
    return (left.astype(f32) + right.astype(f32)).astype(bf16)


def gather_col(part):
    half = jnp.stack([part] + [swap(part, m * X_ONE) for m in (1, 2, 3)])
    near = jnp.concatenate([half, swap(half, Y_HI)])
    return near, swap(near, CORE)


def gather_third(part):
    near = jnp.stack([part] + [swap(part, m * X_ONE) for m in (1, 2, 3)])
    return near, swap(near, CORE)


def fold_kernel(both_ref, got_ref, out_ref):
    half = got_ref.shape[0] // 2
    for m in range(half):
        out_ref[m, 0] = plus(both_ref[m], got_ref[half + m])
        out_ref[m, 1] = plus(both_ref[half + m], got_ref[m])


def fold(both, got):
    slabs, own, rank = got.shape
    return pl.pallas_call(
        fold_kernel,
        in_specs=[pl.BlockSpec(memory_space=pltpu.VMEM)] * 2,
        out_specs=pl.BlockSpec(memory_space=pltpu.VMEM),
        out_shape=jax.ShapeDtypeStruct((slabs // 2, 2, own, rank), bf16),
        compiler_params=pltpu.CompilerParams(vmem_limit_bytes=8 << 20),
        cost_estimate=pl.CostEstimate(flops=1 << 16, bytes_accessed=1 << 18, transcendentals=0),
    )(both, got)


def reduce_col(both):
    pairs = fold(both, swap(both[4:], Y_HI))
    got = [swap(pairs[m], m * X_ONE) for m in (1, 2, 3)]
    out = pairs[0].astype(f32)
    for part in got:
        out = out + part.astype(f32)
    return out[0], out[1]


def shards(
    tensor, loss_kind, factor_one, factor_two, factor_three,
    first_one, second_one, first_two, second_two, first_three, second_three,
):
    tile_rows, tile_depth, tile_cols = tensor.shape
    n_row, n_col = lax.axis_size("row"), lax.axis_size("col")
    rank = factor_one.shape[1]
    own_two = factor_two.shape[0]
    deep = 2 * tile_depth // n_col
    full_rows, full_cols = tile_rows * n_row, tile_cols * n_col
    scales = (
        1.0 / math.sqrt(full_cols * tile_depth),
        1.0 / math.sqrt(full_rows * tile_depth),
        1.0 / math.sqrt(full_rows * full_cols),
    )
    here = lax.axis_index("col")
    ids = jnp.stack([loss_kind[0, 0, 0], here.astype(jnp.int32)])
    mine = lambda x: lax.dynamic_slice_in_dim(x, third_slab(here) * deep, deep, 0)
    part_three, first_three, second_three = mine(factor_three), mine(first_three), mine(second_three)
    start_one, start_two, start_three = (factor_one, factor_two, part_three)
    twos = swap_all(to_all(factor_two.astype(bf16), n_row), "row")
    near, far = gather_col(factor_one.astype(bf16))
    threes = (factor_three.astype(bf16).reshape(tile_depth // deep, deep, rank),)
    for iteration in range(ITERS):
        last = iteration == ITERS - 1
        counter = STEP + iteration + 1
        sent, kept, slope, ones, all_threes = slopes(ids, tensor, near, far, twos, threes, scales)
        grad_two = second_grad(slope, ones, all_threes, scales[1]).reshape(n_row, own_two, rank)
        both = plus(kept, swap(sent, CORE))
        if not last:
            both, grad_two = lax.optimization_barrier((both, grad_two))
        grad_one, grad_three = reduce_col(both)
        factor_one, first_one, second_one = adam_step(factor_one, first_one, second_one, grad_one, counter)
        grad_three = grad_three.astype(bf16)
        if last:
            sent = jnp.concatenate([grad_two, to_all(grad_three, n_row)], axis=1)
            got = total(swap_all(sent, "row"))
            grad_two, grad_three = got[:own_two], got[own_two:]
        else:
            grad_two = total(swap_all(grad_two, "row"))
        factor_two, first_two, second_two = adam_step(factor_two, first_two, second_two, grad_two, counter)
        if not last:
            near, far = gather_col(factor_one.astype(bf16))
            sent = jnp.concatenate([factor_two.astype(bf16), grad_three])
            twos = swap_all(to_all(sent, n_row), "row")
            grad_three = total(twos[:, own_two:])
        part_three, first_three, second_three = adam_step(
            part_three, first_three, second_three, grad_three, counter
        )
        if not last:
            threes = gather_third(part_three.astype(bf16))
    spread = learn_rate * ITERS
    new_three = place_third(ids, *gather_third((start_three - part_three) / spread)).reshape(tile_depth, rank)
    return ((start_one - factor_one) / spread, (start_two - factor_two) / spread, new_three)


def solution(mesh):
    in_specs = (
        P("row", None, "col"),
        P("row", None, "col"),
        P(("row", "col"), None),
        P(("col", "row"), None),
        P(),
        P(("row", "col"), None),
        P(("row", "col"), None),
        P(("col", "row"), None),
        P(("col", "row"), None),
        P(),
        P(),
    )
    out_specs = (P(("row", "col"), None), P(("col", "row"), None), P())
    return jax.shard_map(shards, mesh=mesh, in_specs=in_specs, out_specs=out_specs, check_vma=False)
```

```python
import functools
import math

import jax
import jax.numpy as jnp
from jax import lax
from jax.experimental import pallas as pl
from jax.experimental.pallas import tpu as pltpu
from jax.sharding import PartitionSpec as P

ITERS = 2
STEP = 10
BLOCK = 64
SUB = 4
VMEM_LIMIT = 32 << 20

learn_rate = 0.05
beta_one = 0.8
beta_two = 0.95
adam_eps = 1e-08

f32 = jnp.float32
bf16 = jnp.bfloat16

CORE, Y_HI, X_ONE = 1, 2, 4


def adam_step(param, first, second, grad, counter):
    first = beta_one * first + (1.0 - beta_one) * grad
    second = beta_two * second + (1.0 - beta_two) * grad * grad
    corr_one = 1.0 - beta_one**counter
    corr_two = 1.0 - beta_two**counter
    param = param - learn_rate * (first / corr_one) / (jnp.sqrt(second / corr_two) + adam_eps)
    return (param, first, second)


def gather_codes():
    return [y + x * X_ONE for y in (0, Y_HI) for x in range(4)]


def third_slab(col):
    return col // X_ONE * 2 + col % 2


def slope_kernel(scales, stepped, ids_ref, data_ref, near_ref, far_ref, two_ref, *refs):
    if not stepped:
        three_in_ref, *refs = refs
    sent_ref, kept_ref, slope_ref, one_ref, three_ref, ga_acc, gc_acc = refs
    step = pl.program_id(0)
    n_slab, own, rank = one_ref.shape
    depth = three_ref.shape[0] * three_ref.shape[1]
    cols = two_ref.shape[0] * two_ref.shape[1]
    here = ids_ref[1]

    @pl.when(step == 0)
    def _():
        for place, code in enumerate(gather_codes()):
            one_ref[here ^ code] = near_ref[place]
            one_ref[here ^ code ^ CORE] = far_ref[place]
        if stepped:
            for m in range(4):
                col = here ^ (m * X_ONE)
                three_ref[third_slab(col)] = near_ref[8 + m]
                three_ref[third_slab(col ^ CORE)] = far_ref[8 + m]
        else:
            three_ref[...] = three_in_ref[...]
        gc_acc[...] = jnp.zeros_like(gc_acc)

    def run(logistic):
        two = two_ref[...].reshape(cols, rank)
        three = three_ref[...].reshape(depth, rank)
        three_f = three.astype(f32)
        slabs = BLOCK // own
        one = one_ref[pl.ds(step * slabs, slabs)].reshape(BLOCK, rank)
        n = BLOCK // SUB

        def rows(s):
            return slice(s * SUB, (s + 1) * SUB)

        def rebuild(s):
            scaled = (one[rows(s)][:, None, :] * three[None]).reshape(SUB * depth, rank)
            return lax.dot_general(scaled, two, (((1,), (1,)), ((), ())), preferred_element_type=f32)

        def slope(s, rebuilt):
            values = data_ref[rows(s)].reshape(SUB * depth, cols).astype(f32)
            if logistic:
                out = 0.5 * jnp.tanh(0.5 * rebuilt) + jnp.where(values > 0, -0.5, 0.5)
            else:
                out = jnp.clip(rebuilt - values, -1.0, 1.0)
            out = out.astype(bf16)
            slope_ref[rows(s)] = out.reshape(SUB, depth, cols)
            return out

        def project(deriv):
            return jnp.dot(deriv, two, preferred_element_type=f32).reshape(SUB, depth, rank)

        rebuilt, derivs, projs = {}, {}, {}
        grad_one, grad_three = [], None
        for t in range(n + 3):
            if t < n:
                rebuilt[t] = rebuild(t)
            if 0 <= t - 1 < n:
                derivs[t - 1] = slope(t - 1, rebuilt.pop(t - 1))
            if 0 <= t - 2 < n:
                projs[t - 2] = project(derivs.pop(t - 2))
            if 0 <= t - 3 < n:
                proj = projs.pop(t - 3)
                one_f = one[rows(t - 3)].astype(f32)
                grad_one.append(jnp.sum(proj * three_f[None], axis=1))
                part = jnp.sum(proj * one_f[:, None, :], axis=0)
                grad_three = part if grad_three is None else grad_three + part
        ga_acc[pl.ds(step * slabs, slabs)] = jnp.concatenate(grad_one).reshape(slabs, own, rank)
        gc_acc[...] += grad_three.reshape(gc_acc.shape)

    pl.when(ids_ref[0] == 1)(lambda: run(True))
    pl.when(ids_ref[0] != 1)(lambda: run(False))

    @pl.when(step == pl.num_programs(0) - 1)
    def _():
        for side, out_ref in ((here, kept_ref), (here ^ CORE, sent_ref)):
            for m in range(4):
                col = side ^ (m * X_ONE)
                out_ref[m] = (ga_acc[col] * scales[0]).astype(bf16)
                out_ref[4 + m] = (gc_acc[third_slab(col)] * scales[2]).astype(bf16)
                out_ref[8 + m] = (ga_acc[col ^ Y_HI] * scales[0]).astype(bf16)


def slopes(ids, tensor, near, far, twos, half_three, scales, stepped):
    rows, depth, cols = tensor.shape
    own, rank = near.shape[1:]
    slabs = rows // own
    threes = half_three.shape
    whole = lambda shape: pl.BlockSpec(shape, lambda i: (0,) * len(shape))
    swapped = (12, own, rank)
    return pl.pallas_call(
        functools.partial(slope_kernel, scales, stepped),
        grid=(rows // BLOCK,),
        in_specs=[
            pl.BlockSpec(memory_space=pltpu.SMEM),
            pl.BlockSpec((BLOCK, depth, cols), lambda i: (i, 0, 0)),
            whole(near.shape),
            whole(far.shape),
            whole(twos.shape),
            *([] if stepped else [whole(threes)]),
        ],
        out_specs=[
            whole(swapped),
            whole(swapped),
            pl.BlockSpec((BLOCK, depth, cols), lambda i: (i, 0, 0)),
            whole((slabs, own, rank)),
            whole(threes),
        ],
        out_shape=[
            jax.ShapeDtypeStruct(swapped, bf16),
            jax.ShapeDtypeStruct(swapped, bf16),
            jax.ShapeDtypeStruct((rows, depth, cols), bf16),
            jax.ShapeDtypeStruct((slabs, own, rank), bf16),
            jax.ShapeDtypeStruct(threes, bf16),
        ],
        scratch_shapes=[
            pltpu.VMEM((slabs, own, rank), f32),
            pltpu.VMEM(threes, f32),
        ],
        compiler_params=pltpu.CompilerParams(vmem_limit_bytes=VMEM_LIMIT),
        cost_estimate=pl.CostEstimate(
            flops=8 * rows * depth * cols * rank, bytes_accessed=4 << 20, transcendentals=rows * depth * cols
        ),
    )(ids, tensor, near, far, twos, *([] if stepped else [half_three]))


def second_kernel(scale, slope_ref, one_ref, three_ref, out_ref, acc):
    step = pl.program_id(0)
    block, depth, cols = slope_ref.shape
    rank = one_ref.shape[2]
    one = one_ref[...].reshape(block, rank)
    three = three_ref[...].reshape(depth, rank)
    scaled = (one[:, None, :] * three[None]).reshape(block * depth, rank)
    part = lax.dot_general(
        slope_ref[...].reshape(block * depth, cols), scaled, (((0,), (0,)), ((), ())), preferred_element_type=f32
    )

    @pl.when(step == 0)
    def _():
        acc[...] = part

    @pl.when(step != 0)
    def _():
        acc[...] += part

    @pl.when(step == pl.num_programs(0) - 1)
    def _():
        out_ref[...] = (acc[...] * scale).astype(bf16)


def second_grad(slope, ones, threes, scale):
    rows, depth, cols = slope.shape
    slabs, own, rank = ones.shape
    block = 32
    return pl.pallas_call(
        functools.partial(second_kernel, scale),
        grid=(rows // block,),
        in_specs=[
            pl.BlockSpec((block, depth, cols), lambda i: (i, 0, 0)),
            pl.BlockSpec((block // own, own, rank), lambda i: (i, 0, 0)),
            pl.BlockSpec(threes.shape, lambda i: (0, 0, 0)),
        ],
        out_specs=pl.BlockSpec((cols, rank), lambda i: (0, 0)),
        out_shape=jax.ShapeDtypeStruct((cols, rank), bf16),
        scratch_shapes=[pltpu.VMEM((cols, rank), f32)],
        compiler_params=pltpu.CompilerParams(vmem_limit_bytes=VMEM_LIMIT),
        cost_estimate=pl.CostEstimate(
            flops=4 * rows * depth * cols * rank, bytes_accessed=2 << 20, transcendentals=0
        ),
    )(slope, ones, threes)


def place_kernel(ids_ref, near_ref, far_ref, out_ref):
    for m in range(4):
        col = ids_ref[1] ^ (m * X_ONE)
        out_ref[third_slab(col)] = near_ref[m]
        out_ref[third_slab(col ^ CORE)] = far_ref[m]


def place_third(ids, near, far):
    slabs, own, rank = near.shape
    return pl.pallas_call(
        place_kernel,
        in_specs=[pl.BlockSpec(memory_space=pltpu.SMEM)] + [pl.BlockSpec(memory_space=pltpu.VMEM)] * 2,
        out_specs=pl.BlockSpec(memory_space=pltpu.VMEM),
        out_shape=jax.ShapeDtypeStruct((2 * slabs, own, rank), near.dtype),
        compiler_params=pltpu.CompilerParams(vmem_limit_bytes=8 << 20),
    )(ids, near, far)


def swap_all(parts, axis):
    return lax.all_to_all(parts, axis, 0, 0)


def to_all(part, size):
    return jnp.broadcast_to(part[None], (size,) + part.shape)


def total(parts):
    return jnp.sum(parts.astype(f32), axis=0)


def swap(part, code):
    size = lax.axis_size("col")
    return lax.ppermute(part, "col", [(i, i ^ code) for i in range(size)])


def plus(left, right):
    return (left.astype(f32) + right.astype(f32)).astype(bf16)


def gather_x(part):
    return jnp.stack([part] + [swap(part, m * X_ONE) for m in (1, 2, 3)])


def gather_first(part):
    half = gather_x(part)
    near = jnp.concatenate([half, swap(half, Y_HI)])
    return near, swap(near, CORE)


def gather_both(part_one, part_three):
    half = gather_x(jnp.stack([part_one, part_three]))
    near = jnp.concatenate([half[:, 0], swap(half[:, 0], Y_HI), half[:, 1]])
    return near, swap(near, CORE)


def fold_kernel(both_ref, got_ref, out_ref):
    half = got_ref.shape[0] // 2
    for m in range(half):
        out_ref[m, 0] = plus(both_ref[m], got_ref[half + m])
        out_ref[m, 1] = plus(both_ref[half + m], got_ref[m])


def fold(both, got):
    slabs, own, rank = got.shape
    return pl.pallas_call(
        fold_kernel,
        in_specs=[pl.BlockSpec(memory_space=pltpu.VMEM)] * 2,
        out_specs=pl.BlockSpec(memory_space=pltpu.VMEM),
        out_shape=jax.ShapeDtypeStruct((slabs // 2, 2, own, rank), bf16),
        compiler_params=pltpu.CompilerParams(vmem_limit_bytes=8 << 20),
        cost_estimate=pl.CostEstimate(flops=1 << 16, bytes_accessed=1 << 18, transcendentals=0),
    )(both, got)


def reduce_col(both):
    pairs = fold(both, swap(both[4:], Y_HI))
    got = [swap(pairs[m], m * X_ONE) for m in (1, 2, 3)]
    out = pairs[0].astype(f32)
    for part in got:
        out = out + part.astype(f32)
    return out[0], out[1]


def shards(
    tensor, loss_kind, factor_one, factor_two, factor_three,
    first_one, second_one, first_two, second_two, first_three, second_three,
):
    tile_rows, tile_depth, tile_cols = tensor.shape
    n_row, n_col = lax.axis_size("row"), lax.axis_size("col")
    rank = factor_one.shape[1]
    own_two = factor_two.shape[0]
    deep = 2 * tile_depth // n_col
    full_rows, full_cols = tile_rows * n_row, tile_cols * n_col
    scales = (
        1.0 / math.sqrt(full_cols * tile_depth),
        1.0 / math.sqrt(full_rows * tile_depth),
        1.0 / math.sqrt(full_rows * full_cols),
    )
    here = lax.axis_index("col")
    ids = jnp.stack([loss_kind[0, 0, 0], here.astype(jnp.int32)])
    mine = lambda x: lax.dynamic_slice_in_dim(x, third_slab(here) * deep, deep, 0)
    part_three, first_three, second_three = mine(factor_three), mine(first_three), mine(second_three)
    start_one, start_two, start_three = (factor_one, factor_two, part_three)
    twos = swap_all(to_all(factor_two.astype(bf16), n_row), "row")
    near, far = gather_first(factor_one.astype(bf16))
    threes = factor_three.astype(bf16).reshape(tile_depth // deep, deep, rank)
    for iteration in range(ITERS):
        counter = STEP + iteration + 1
        sent, kept, slope, ones, threes = slopes(
            ids, tensor, near, far, twos, threes, scales, iteration > 0
        )
        grad_two = second_grad(slope, ones, threes, scales[1]).reshape(n_row, own_two, rank)
        grad_one, grad_three = reduce_col(plus(kept, swap(sent, CORE)))
        sent = jnp.concatenate([grad_two, to_all(grad_three.astype(bf16), n_row)], axis=1)
        factor_one, first_one, second_one = adam_step(factor_one, first_one, second_one, grad_one, counter)
        got = total(swap_all(sent, "row"))
        grad_two, grad_three = got[:own_two], got[own_two:]
        part_three, first_three, second_three = adam_step(
            part_three, first_three, second_three, grad_three, counter
        )
        if iteration < ITERS - 1:
            near, far = gather_both(factor_one.astype(bf16), part_three.astype(bf16))
        else:
            near = gather_x((start_three - part_three) / (learn_rate * ITERS))
            near, grad_two = lax.optimization_barrier((near, grad_two))
        factor_two, first_two, second_two = adam_step(factor_two, first_two, second_two, grad_two, counter)
        if iteration < ITERS - 1:
            twos = swap_all(to_all(factor_two.astype(bf16), n_row), "row")
    spread = learn_rate * ITERS
    new_three = place_third(ids, near, swap(near, CORE)).reshape(tile_depth, rank)
    return ((start_one - factor_one) / spread, (start_two - factor_two) / spread, new_three)


def solution(mesh):
    in_specs = (
        P("row", None, "col"),
        P("row", None, "col"),
        P(("row", "col"), None),
        P(("col", "row"), None),
        P(),
        P(("row", "col"), None),
        P(("row", "col"), None),
        P(("col", "row"), None),
        P(("col", "row"), None),
        P(),
        P(),
    )
    out_specs = (P(("row", "col"), None), P(("col", "row"), None), P())
    return jax.shard_map(shards, mesh=mesh, in_specs=in_specs, out_specs=out_specs, check_vma=False)
```

```python
import functools
import math

import jax
import jax.numpy as jnp
from jax import lax
from jax.experimental import pallas as pl
from jax.experimental.pallas import tpu as pltpu
from jax.sharding import PartitionSpec as P

ITERS = 2
STEP = 10
BLOCK = 64
SUB = 4
VMEM_LIMIT = 50 << 20

learn_rate = 0.05
beta_one = 0.8
beta_two = 0.95
adam_eps = 1e-08

f32 = jnp.float32
bf16 = jnp.bfloat16

CORE, Y_HI, X_ONE = 1, 2, 4


def adam_step(param, first, second, grad, counter):
    first = beta_one * first + (1.0 - beta_one) * grad
    second = beta_two * second + (1.0 - beta_two) * grad * grad
    corr_one = 1.0 - beta_one**counter
    corr_two = 1.0 - beta_two**counter
    param = param - learn_rate * (first / corr_one) / (jnp.sqrt(second / corr_two) + adam_eps)
    return (param, first, second)


def third_slab(col):
    return col // X_ONE * 2 + col % 2


def slope_kernel(scales, stepped, ids_ref, data_ref, two_ref, near_ref, near_y_ref, far_ref, far_y_ref, *refs):
    if stepped:
        near_three_ref, far_three_ref, *refs = refs
    else:
        three_in_ref, *refs = refs
    sent_ref, kept_ref, slope_ref, one_ref, three_ref, ga_acc, gc_acc = refs
    step = pl.program_id(0)
    n_slab, own, rank = one_ref.shape
    depth = three_ref.shape[0] * three_ref.shape[1]
    cols = two_ref.shape[0] * two_ref.shape[1]
    here = ids_ref[0] // 2

    @pl.when(step == 0)
    def _():
        for m in range(4):
            col = here ^ (m * X_ONE)
            one_ref[col] = near_ref[m]
            one_ref[col ^ Y_HI] = near_y_ref[m]
            one_ref[col ^ CORE] = far_ref[m]
            one_ref[col ^ CORE ^ Y_HI] = far_y_ref[m]
            if stepped:
                three_ref[third_slab(col)] = near_three_ref[m]
                three_ref[third_slab(col ^ CORE)] = far_three_ref[m]
        if not stepped:
            three_ref[...] = three_in_ref[...].astype(bf16)
        gc_acc[...] = jnp.zeros_like(gc_acc)

    def run(logistic):
        two = two_ref[...].reshape(cols, rank)
        three = three_ref[...].reshape(depth, rank)
        three_f = three.astype(f32)
        slabs = BLOCK // own
        one = one_ref[pl.ds(step * slabs, slabs)].reshape(BLOCK, rank)
        n = BLOCK // SUB

        def rows(s):
            return slice(s * SUB, (s + 1) * SUB)

        def rebuild(s):
            scaled = (one[rows(s)][:, None, :] * three[None]).reshape(SUB * depth, rank)
            return lax.dot_general(scaled, two, (((1,), (1,)), ((), ())), preferred_element_type=f32)

        def slope(s, rebuilt):
            values = data_ref[rows(s)].reshape(SUB * depth, cols).astype(f32)
            if logistic:
                out = 0.5 * jnp.tanh(0.5 * rebuilt) + jnp.where(values > 0, -0.5, 0.5)
            else:
                out = jnp.clip(rebuilt - values, -1.0, 1.0)
            out = out.astype(bf16)
            slope_ref[rows(s)] = out.reshape(SUB, depth, cols)
            return out

        def project(deriv):
            return jnp.dot(deriv, two, preferred_element_type=f32).reshape(SUB, depth, rank)

        rebuilt, derivs, projs = {}, {}, {}
        grad_one, grad_three = [], None
        for t in range(n + 3):
            if t < n:
                rebuilt[t] = rebuild(t)
            if 0 <= t - 1 < n:
                derivs[t - 1] = slope(t - 1, rebuilt.pop(t - 1))
            if 0 <= t - 2 < n:
                projs[t - 2] = project(derivs.pop(t - 2))
            if 0 <= t - 3 < n:
                proj = projs.pop(t - 3)
                one_f = one[rows(t - 3)].astype(f32)
                grad_one.append(jnp.sum(proj * three_f[None], axis=1))
                part = jnp.sum(proj * one_f[:, None, :], axis=0)
                grad_three = part if grad_three is None else grad_three + part
        ga_acc[pl.ds(step * slabs, slabs)] = jnp.concatenate(grad_one).reshape(slabs, own, rank)
        gc_acc[...] += grad_three.reshape(gc_acc.shape)

    pl.when(ids_ref[0] % 2 == 1)(lambda: run(True))
    pl.when(ids_ref[0] % 2 != 1)(lambda: run(False))

    @pl.when(step == pl.num_programs(0) - 1)
    def _():
        for side, out_ref in ((here, kept_ref), (here ^ CORE, sent_ref)):
            for m in range(4):
                col = side ^ (m * X_ONE)
                out_ref[m] = (ga_acc[col] * scales[0]).astype(bf16)
                out_ref[4 + m] = (gc_acc[third_slab(col)] * scales[2]).astype(bf16)
                out_ref[8 + m] = (ga_acc[col ^ Y_HI] * scales[0]).astype(bf16)


def slopes(ids, tensor, twos, ones, threes, scales):
    rows, depth, cols = tensor.shape
    own, rank = ones[0].shape[1:]
    slabs = rows // own
    stepped = len(threes) == 2
    all_threes = (depth // threes[0].shape[1],) + threes[0].shape[1:]
    whole = lambda shape: pl.BlockSpec(shape, lambda i: (0,) * len(shape))
    swapped = (12, own, rank)
    return pl.pallas_call(
        functools.partial(slope_kernel, scales, stepped),
        grid=(rows // BLOCK,),
        in_specs=[
            pl.BlockSpec(memory_space=pltpu.SMEM),
            pl.BlockSpec((BLOCK, depth, cols), lambda i: (i, 0, 0)),
            *[whole(x.shape) for x in (twos, *ones, *threes)],
        ],
        out_specs=[
            whole(swapped),
            whole(swapped),
            pl.BlockSpec((BLOCK, depth, cols), lambda i: (i, 0, 0)),
            whole((slabs, own, rank)),
            whole(all_threes),
        ],
        out_shape=[
            jax.ShapeDtypeStruct(swapped, bf16),
            jax.ShapeDtypeStruct(swapped, bf16),
            jax.ShapeDtypeStruct((rows, depth, cols), bf16),
            jax.ShapeDtypeStruct((slabs, own, rank), bf16),
            jax.ShapeDtypeStruct(all_threes, bf16),
        ],
        scratch_shapes=[
            pltpu.VMEM((slabs, own, rank), f32),
            pltpu.VMEM(all_threes, f32),
        ],
        compiler_params=pltpu.CompilerParams(vmem_limit_bytes=VMEM_LIMIT),
        cost_estimate=pl.CostEstimate(
            flops=8 * rows * depth * cols * rank, bytes_accessed=4 << 20, transcendentals=rows * depth * cols
        ),
    )(ids, tensor, twos, *ones, *threes)


def second_kernel(scale, slope_ref, one_ref, three_ref, out_ref, acc):
    step = pl.program_id(0)
    block, depth, cols = slope_ref.shape
    rank = one_ref.shape[2]
    one = one_ref[...].reshape(block, rank)
    three = three_ref[...].reshape(depth, rank)
    scaled = (one[:, None, :] * three[None]).reshape(block * depth, rank)
    part = lax.dot_general(
        slope_ref[...].reshape(block * depth, cols), scaled, (((0,), (0,)), ((), ())), preferred_element_type=f32
    )

    @pl.when(step == 0)
    def _():
        acc[...] = part

    @pl.when(step != 0)
    def _():
        acc[...] += part

    @pl.when(step == pl.num_programs(0) - 1)
    def _():
        out_ref[...] = (acc[...] * scale).astype(bf16)


def second_grad(slope, ones, threes, scale):
    rows, depth, cols = slope.shape
    slabs, own, rank = ones.shape
    block = 32
    return pl.pallas_call(
        functools.partial(second_kernel, scale),
        grid=(rows // block,),
        in_specs=[
            pl.BlockSpec((block, depth, cols), lambda i: (i, 0, 0)),
            pl.BlockSpec((block // own, own, rank), lambda i: (i, 0, 0)),
            pl.BlockSpec(threes.shape, lambda i: (0, 0, 0)),
        ],
        out_specs=pl.BlockSpec((cols, rank), lambda i: (0, 0)),
        out_shape=jax.ShapeDtypeStruct((cols, rank), bf16),
        scratch_shapes=[pltpu.VMEM((cols, rank), f32)],
        compiler_params=pltpu.CompilerParams(vmem_limit_bytes=VMEM_LIMIT),
        cost_estimate=pl.CostEstimate(
            flops=4 * rows * depth * cols * rank, bytes_accessed=2 << 20, transcendentals=0
        ),
    )(slope, ones, threes)


def place_kernel(ids_ref, near_ref, far_ref, out_ref):
    for m in range(4):
        col = ids_ref[0] // 2 ^ (m * X_ONE)
        out_ref[third_slab(col)] = near_ref[m]
        out_ref[third_slab(col ^ CORE)] = far_ref[m]


def place_third(ids, near, far):
    slabs, own, rank = near.shape
    return pl.pallas_call(
        place_kernel,
        in_specs=[pl.BlockSpec(memory_space=pltpu.SMEM)] + [pl.BlockSpec(memory_space=pltpu.VMEM)] * 2,
        out_specs=pl.BlockSpec(memory_space=pltpu.VMEM),
        out_shape=jax.ShapeDtypeStruct((2 * slabs, own, rank), near.dtype),
        compiler_params=pltpu.CompilerParams(vmem_limit_bytes=8 << 20),
    )(ids, near, far)


def swap_all(parts, axis):
    return lax.all_to_all(parts, axis, 0, 0)


def to_all(part, size):
    return jnp.broadcast_to(part[None], (size,) + part.shape)


def total(parts):
    return jnp.sum(parts.astype(f32), axis=0)


def swap(part, code):
    size = lax.axis_size("col")
    return lax.ppermute(part, "col", [(i, i ^ code) for i in range(size)])


def plus(left, right):
    return (left.astype(f32) + right.astype(f32)).astype(bf16)


def gather_x(part):
    return jnp.stack([part] + [swap(part, m * X_ONE) for m in (1, 2, 3)])


def fold_kernel(both_ref, got_ref, out_ref):
    half = got_ref.shape[0] // 2
    for m in range(half):
        out_ref[m, 0] = plus(both_ref[m], got_ref[half + m])
        out_ref[m, 1] = plus(both_ref[half + m], got_ref[m])


def fold(both, got):
    slabs, own, rank = got.shape
    return pl.pallas_call(
        fold_kernel,
        in_specs=[pl.BlockSpec(memory_space=pltpu.VMEM)] * 2,
        out_specs=pl.BlockSpec(memory_space=pltpu.VMEM),
        out_shape=jax.ShapeDtypeStruct((slabs // 2, 2, own, rank), bf16),
        compiler_params=pltpu.CompilerParams(vmem_limit_bytes=8 << 20),
        cost_estimate=pl.CostEstimate(flops=1 << 16, bytes_accessed=1 << 18, transcendentals=0),
    )(both, got)


def reduce_col(both):
    pairs = fold(both, swap(both[4:], Y_HI))
    got = [swap(pairs[m], m * X_ONE) for m in (1, 2, 3)]
    out = pairs[0].astype(f32)
    for part in got:
        out = out + part.astype(f32)
    return out[0], out[1]


def shards(
    tensor, loss_kind, factor_one, factor_two, factor_three,
    first_one, second_one, first_two, second_two, first_three, second_three,
):
    tile_rows, tile_depth, tile_cols = tensor.shape
    n_row, n_col = lax.axis_size("row"), lax.axis_size("col")
    rank = factor_one.shape[1]
    own_two = factor_two.shape[0]
    deep = 2 * tile_depth // n_col
    full_rows, full_cols = tile_rows * n_row, tile_cols * n_col
    scales = (
        1.0 / math.sqrt(full_cols * tile_depth),
        1.0 / math.sqrt(full_rows * tile_depth),
        1.0 / math.sqrt(full_rows * full_cols),
    )
    here = lax.axis_index("col")
    ids = loss_kind[0, 0, :1] + 2 * here
    mine = lambda x: lax.dynamic_slice_in_dim(x, third_slab(here) * deep, deep, 0)
    part_three, first_three, second_three = mine(factor_three), mine(first_three), mine(second_three)
    start_one, start_two, start_three = (factor_one, factor_two, part_three)
    twos = swap_all(to_all(factor_two.astype(bf16), n_row), "row")
    near = gather_x(factor_one.astype(bf16))
    near_y = swap(near, Y_HI)
    ones = (near, near_y, swap(near, CORE), swap(near_y, CORE))
    threes = (factor_three.reshape(tile_depth // deep, deep, rank),)
    for iteration in range(ITERS):
        last = iteration == ITERS - 1
        counter = STEP + iteration + 1
        sent, kept, slope, all_ones, all_threes = slopes(ids, tensor, twos, ones, threes, scales)
        grad_two = second_grad(slope, all_ones, all_threes, scales[1]).reshape(n_row, own_two, rank)
        grad_one, grad_three = reduce_col(plus(kept, swap(sent, CORE)))
        sent = jnp.concatenate([grad_two, to_all(grad_three.astype(bf16), n_row)], axis=1)
        factor_one, first_one, second_one = adam_step(factor_one, first_one, second_one, grad_one, counter)
        got = swap_all(sent, "row")
        if not last:
            near = gather_x(factor_one.astype(bf16))
            got, near = lax.optimization_barrier((got, near))
            near_y = swap(near, Y_HI)
        got = total(got)
        grad_two, grad_three = got[:own_two], got[own_two:]
        part_three, first_three, second_three = adam_step(
            part_three, first_three, second_three, grad_three, counter
        )
        if last:
            near = gather_x((start_three - part_three) / (learn_rate * ITERS))
            near, grad_two = lax.optimization_barrier((near, grad_two))
        factor_two, first_two, second_two = adam_step(factor_two, first_two, second_two, grad_two, counter)
        if not last:
            near_three = gather_x(part_three.astype(bf16))
            twos = swap_all(to_all(factor_two.astype(bf16), n_row), "row")
            twos, near_y, near_three = lax.optimization_barrier((twos, near_y, near_three))
            ones = (near, near_y, swap(near, CORE), swap(near_y, CORE))
            threes = (near_three, swap(near_three, CORE))
    spread = learn_rate * ITERS
    new_three = place_third(ids, near, swap(near, CORE)).reshape(tile_depth, rank)
    return ((start_one - factor_one) / spread, (start_two - factor_two) / spread, new_three)


def solution(mesh):
    in_specs = (
        P("row", None, "col"),
        P("row", None, "col"),
        P(("row", "col"), None),
        P(("col", "row"), None),
        P(),
        P(("row", "col"), None),
        P(("row", "col"), None),
        P(("col", "row"), None),
        P(("col", "row"), None),
        P(),
        P(),
    )
    out_specs = (P(("row", "col"), None), P(("col", "row"), None), P())
    return jax.shard_map(shards, mesh=mesh, in_specs=in_specs, out_specs=out_specs, check_vma=False)
```

```python
import functools
import math

import jax
import jax.numpy as jnp
from jax import lax
from jax.experimental import pallas as pl
from jax.experimental.pallas import tpu as pltpu
from jax.sharding import PartitionSpec as P

ITERS = 2
STEP = 10
BLOCK = 64
SUB = 4
VMEM_LIMIT = 50 << 20
VMEM_ALL = 61 << 20
VMEM_LATER = 32 << 20

learn_rate = 0.05
beta_one = 0.8
beta_two = 0.95
adam_eps = 1e-08

f32 = jnp.float32
bf16 = jnp.bfloat16

CORE, Y_HI, X_ONE = 1, 2, 4


def adam_step(param, first, second, grad, counter):
    first = beta_one * first + (1.0 - beta_one) * grad
    second = beta_two * second + (1.0 - beta_two) * grad * grad
    corr_one = 1.0 - beta_one**counter
    corr_two = 1.0 - beta_two**counter
    param = param - learn_rate * (first / corr_one) / (jnp.sqrt(second / corr_two) + adam_eps)
    return (param, first, second)


def third_slab(col):
    return col // X_ONE * 2 + col % 2


def slope_kernel(scales, stepped, ids_ref, data_ref, two_ref, near_ref, near_y_ref, far_ref, far_y_ref, *refs):
    if stepped:
        near_three_ref, far_three_ref, *refs = refs
    else:
        three_in_ref, *refs = refs
    sent_ref, kept_ref, slope_ref, one_ref, three_ref, ga_acc, gc_acc = refs
    step = pl.program_id(0)
    n_slab, own, rank = one_ref.shape
    depth = three_ref.shape[0] * three_ref.shape[1]
    cols = two_ref.shape[0] * two_ref.shape[1]
    here = ids_ref[0] // 2

    @pl.when(step == 0)
    def _():
        for m in range(4):
            col = here ^ (m * X_ONE)
            one_ref[col] = near_ref[m]
            one_ref[col ^ Y_HI] = near_y_ref[m]
            one_ref[col ^ CORE] = far_ref[m]
            one_ref[col ^ CORE ^ Y_HI] = far_y_ref[m]
            if stepped:
                three_ref[third_slab(col)] = near_three_ref[m]
                three_ref[third_slab(col ^ CORE)] = far_three_ref[m]
        if not stepped:
            three_ref[...] = three_in_ref[...]
        gc_acc[...] = jnp.zeros_like(gc_acc)

    def run(logistic):
        two = two_ref[...].reshape(cols, rank)
        three = three_ref[...].reshape(depth, rank)
        three_f = three.astype(f32)
        slabs = BLOCK // own
        one = one_ref[pl.ds(step * slabs, slabs)].reshape(BLOCK, rank)
        n = BLOCK // SUB

        def rows(s):
            return slice(s * SUB, (s + 1) * SUB)

        def rebuild(s):
            scaled = (one[rows(s)][:, None, :] * three[None]).reshape(SUB * depth, rank)
            return lax.dot_general(scaled, two, (((1,), (1,)), ((), ())), preferred_element_type=f32)

        def slope(s, rebuilt):
            values = data_ref[rows(s)].reshape(SUB * depth, cols).astype(f32)
            if logistic:
                out = 0.5 * jnp.tanh(0.5 * rebuilt) + jnp.where(values > 0, -0.5, 0.5)
            else:
                out = jnp.clip(rebuilt - values, -1.0, 1.0)
            out = out.astype(bf16)
            slope_ref[rows(s)] = out.reshape(SUB, depth, cols)
            return out

        def project(deriv):
            return jnp.dot(deriv, two, preferred_element_type=f32).reshape(SUB, depth, rank)

        rebuilt, derivs, projs = {}, {}, {}
        grad_one, grad_three = [], None
        for t in range(n + 3):
            if t < n:
                rebuilt[t] = rebuild(t)
            if 0 <= t - 1 < n:
                derivs[t - 1] = slope(t - 1, rebuilt.pop(t - 1))
            if 0 <= t - 2 < n:
                projs[t - 2] = project(derivs.pop(t - 2))
            if 0 <= t - 3 < n:
                proj = projs.pop(t - 3)
                one_f = one[rows(t - 3)].astype(f32)
                grad_one.append(jnp.sum(proj * three_f[None], axis=1))
                part = jnp.sum(proj * one_f[:, None, :], axis=0)
                grad_three = part if grad_three is None else grad_three + part
        ga_acc[pl.ds(step * slabs, slabs)] = jnp.concatenate(grad_one).reshape(slabs, own, rank)
        gc_acc[...] += grad_three.reshape(gc_acc.shape)

    pl.when(ids_ref[0] % 2 == 1)(lambda: run(True))
    pl.when(ids_ref[0] % 2 != 1)(lambda: run(False))

    @pl.when(step == pl.num_programs(0) - 1)
    def _():
        for side, out_ref in ((here, kept_ref), (here ^ CORE, sent_ref)):
            for m in range(4):
                col = side ^ (m * X_ONE)
                out_ref[m] = (ga_acc[col] * scales[0]).astype(bf16)
                out_ref[4 + m] = (gc_acc[third_slab(col)] * scales[2]).astype(bf16)
                out_ref[8 + m] = (ga_acc[col ^ Y_HI] * scales[0]).astype(bf16)


def slopes(ids, tensor, twos, ones, threes, scales):
    rows, depth, cols = tensor.shape
    own, rank = ones[0].shape[1:]
    slabs = rows // own
    stepped = len(threes) == 2
    all_threes = (depth // threes[0].shape[1],) + threes[0].shape[1:]
    whole = lambda shape: pl.BlockSpec(shape, lambda i: (0,) * len(shape))
    swapped = (12, own, rank)
    return pl.pallas_call(
        functools.partial(slope_kernel, scales, stepped),
        grid=(rows // BLOCK,),
        in_specs=[
            pl.BlockSpec(memory_space=pltpu.SMEM),
            pl.BlockSpec((BLOCK, depth, cols), lambda i: (i, 0, 0)),
            *[whole(x.shape) for x in (twos, *ones, *threes)],
        ],
        out_specs=[
            whole(swapped),
            whole(swapped),
            pl.BlockSpec((BLOCK, depth, cols), lambda i: (i, 0, 0)),
            whole((slabs, own, rank)),
            whole(all_threes),
        ],
        out_shape=[
            jax.ShapeDtypeStruct(swapped, bf16),
            jax.ShapeDtypeStruct(swapped, bf16),
            jax.ShapeDtypeStruct((rows, depth, cols), bf16),
            jax.ShapeDtypeStruct((slabs, own, rank), bf16),
            jax.ShapeDtypeStruct(all_threes, bf16),
        ],
        scratch_shapes=[
            pltpu.VMEM((slabs, own, rank), f32),
            pltpu.VMEM(all_threes, f32),
        ],
        compiler_params=pltpu.CompilerParams(vmem_limit_bytes=VMEM_LATER if stepped else VMEM_LIMIT),
        cost_estimate=pl.CostEstimate(
            flops=8 * rows * depth * cols * rank, bytes_accessed=4 << 20, transcendentals=rows * depth * cols
        ),
    )(ids, tensor, twos, *ones, *threes)


def second_kernel(scale, slope_ref, one_ref, three_ref, out_ref, acc):
    step = pl.program_id(0)
    block, depth, cols = slope_ref.shape
    rank = one_ref.shape[2]
    one = one_ref[...].reshape(block, rank)
    three = three_ref[...].reshape(depth, rank)
    scaled = (one[:, None, :] * three[None]).reshape(block * depth, rank)
    part = lax.dot_general(
        slope_ref[...].reshape(block * depth, cols), scaled, (((0,), (0,)), ((), ())), preferred_element_type=f32
    )

    @pl.when(step == 0)
    def _():
        acc[...] = part

    @pl.when(step != 0)
    def _():
        acc[...] += part

    @pl.when(step == pl.num_programs(0) - 1)
    def _():
        out_ref[...] = (acc[...] * scale).astype(bf16)


def second_grad(slope, ones, threes, scale):
    rows, depth, cols = slope.shape
    slabs, own, rank = ones.shape
    block = 32
    return pl.pallas_call(
        functools.partial(second_kernel, scale),
        grid=(rows // block,),
        in_specs=[
            pl.BlockSpec((block, depth, cols), lambda i: (i, 0, 0)),
            pl.BlockSpec((block // own, own, rank), lambda i: (i, 0, 0)),
            pl.BlockSpec(threes.shape, lambda i: (0, 0, 0)),
        ],
        out_specs=pl.BlockSpec((cols, rank), lambda i: (0, 0)),
        out_shape=jax.ShapeDtypeStruct((cols, rank), bf16),
        scratch_shapes=[pltpu.VMEM((cols, rank), f32)],
        compiler_params=pltpu.CompilerParams(vmem_limit_bytes=VMEM_LIMIT),
        cost_estimate=pl.CostEstimate(
            flops=4 * rows * depth * cols * rank, bytes_accessed=2 << 20, transcendentals=0
        ),
    )(slope, ones, threes)


def prepare_kernel(kind_ref, two_ref, three_ref, ids_ref, twos_ref, half_three_ref):
    ids_ref[0] = kind_ref[0, 0, 0] + 2 * lax.axis_index("col")
    two = two_ref[...].astype(bf16)
    for slab in range(twos_ref.shape[0]):
        twos_ref[slab] = two
    half_three_ref[...] = three_ref[...].astype(bf16)


def prepare(loss_kind, two, three, copies):
    whole = lambda shape: pl.BlockSpec(shape, lambda i: (0,) * len(shape))
    return pl.pallas_call(
        prepare_kernel,
        grid=(1,),
        in_specs=[
            pl.BlockSpec((1, 8, 128), lambda i: (0, 0, 0), memory_space=pltpu.SMEM),
            whole(two.shape),
            whole(three.shape),
        ],
        out_specs=[
            pl.BlockSpec(memory_space=pltpu.SMEM),
            whole((copies,) + two.shape),
            whole(three.shape),
        ],
        out_shape=[
            jax.ShapeDtypeStruct((1,), jnp.int32),
            jax.ShapeDtypeStruct((copies,) + two.shape, bf16),
            jax.ShapeDtypeStruct(three.shape, bf16),
        ],
        compiler_params=pltpu.CompilerParams(vmem_limit_bytes=VMEM_ALL),
    )(loss_kind, two, three)


def place_kernel(ids_ref, near_ref, far_ref, out_ref):
    for m in range(4):
        col = ids_ref[0] // 2 ^ (m * X_ONE)
        out_ref[third_slab(col)] = near_ref[m]
        out_ref[third_slab(col ^ CORE)] = far_ref[m]


def place_third(ids, near, far):
    slabs, own, rank = near.shape
    return pl.pallas_call(
        place_kernel,
        in_specs=[pl.BlockSpec(memory_space=pltpu.SMEM)] + [pl.BlockSpec(memory_space=pltpu.VMEM)] * 2,
        out_specs=pl.BlockSpec(memory_space=pltpu.VMEM),
        out_shape=jax.ShapeDtypeStruct((2 * slabs, own, rank), near.dtype),
        compiler_params=pltpu.CompilerParams(vmem_limit_bytes=8 << 20),
    )(ids, near, far)


def swap_all(parts, axis):
    return lax.all_to_all(parts, axis, 0, 0)


def to_all(part, size):
    return jnp.broadcast_to(part[None], (size,) + part.shape)


def total(parts):
    return jnp.sum(parts.astype(f32), axis=0)


def swap(part, code):
    size = lax.axis_size("col")
    return lax.ppermute(part, "col", [(i, i ^ code) for i in range(size)])


def plus(left, right):
    return (left.astype(f32) + right.astype(f32)).astype(bf16)


def gather_x(part):
    return jnp.stack([part] + [swap(part, m * X_ONE) for m in (1, 2, 3)])


def fold_kernel(both_ref, got_ref, out_ref):
    half = got_ref.shape[0] // 2
    for m in range(half):
        out_ref[m, 0] = plus(both_ref[m], got_ref[half + m])
        out_ref[m, 1] = plus(both_ref[half + m], got_ref[m])


def fold(both, got):
    slabs, own, rank = got.shape
    return pl.pallas_call(
        fold_kernel,
        in_specs=[pl.BlockSpec(memory_space=pltpu.VMEM)] * 2,
        out_specs=pl.BlockSpec(memory_space=pltpu.VMEM),
        out_shape=jax.ShapeDtypeStruct((slabs // 2, 2, own, rank), bf16),
        compiler_params=pltpu.CompilerParams(vmem_limit_bytes=8 << 20),
        cost_estimate=pl.CostEstimate(flops=1 << 16, bytes_accessed=1 << 18, transcendentals=0),
    )(both, got)


def reduce_col(both):
    pairs = fold(both, swap(both[4:], Y_HI))
    got = [swap(pairs[m], m * X_ONE) for m in (1, 2, 3)]
    out = pairs[0].astype(f32)
    for part in got:
        out = out + part.astype(f32)
    return out[0], out[1]


def shards(
    tensor, loss_kind, factor_one, factor_two, factor_three,
    first_one, second_one, first_two, second_two, first_three, second_three,
):
    tile_rows, tile_depth, tile_cols = tensor.shape
    n_row, n_col = lax.axis_size("row"), lax.axis_size("col")
    rank = factor_one.shape[1]
    own_two = factor_two.shape[0]
    deep = 2 * tile_depth // n_col
    full_rows, full_cols = tile_rows * n_row, tile_cols * n_col
    scales = (
        1.0 / math.sqrt(full_cols * tile_depth),
        1.0 / math.sqrt(full_rows * tile_depth),
        1.0 / math.sqrt(full_rows * full_cols),
    )
    here = lax.axis_index("col")
    mine = lambda x: lax.dynamic_slice_in_dim(x, third_slab(here) * deep, deep, 0)
    part_three, first_three, second_three = mine(factor_three), mine(first_three), mine(second_three)
    start_one, start_two, start_three = (factor_one, factor_two, part_three)
    threes = factor_three.reshape(tile_depth // deep, deep, rank)
    ids, sent, threes = prepare(loss_kind, factor_two, threes, n_row)
    twos = swap_all(sent, "row")
    near = gather_x(factor_one.astype(bf16))
    near_y = swap(near, Y_HI)
    ones = (near, near_y, swap(near, CORE), swap(near_y, CORE))
    threes = (threes,)
    for iteration in range(ITERS):
        last = iteration == ITERS - 1
        counter = STEP + iteration + 1
        sent, kept, slope, all_ones, all_threes = slopes(ids, tensor, twos, ones, threes, scales)
        grad_two = second_grad(slope, all_ones, all_threes, scales[1]).reshape(n_row, own_two, rank)
        grad_one, grad_three = reduce_col(plus(kept, swap(sent, CORE)))
        sent = jnp.concatenate([grad_two, to_all(grad_three.astype(bf16), n_row)], axis=1)
        factor_one, first_one, second_one = adam_step(factor_one, first_one, second_one, grad_one, counter)
        got = swap_all(sent, "row")
        if not last:
            near = gather_x(factor_one.astype(bf16))
            got, near = lax.optimization_barrier((got, near))
            near_y = swap(near, Y_HI)
        got = total(got)
        grad_two, grad_three = got[:own_two], got[own_two:]
        part_three, first_three, second_three = adam_step(
            part_three, first_three, second_three, grad_three, counter
        )
        if last:
            near = gather_x((start_three - part_three) / (learn_rate * ITERS))
            near, grad_two = lax.optimization_barrier((near, grad_two))
        factor_two, first_two, second_two = adam_step(factor_two, first_two, second_two, grad_two, counter)
        if not last:
            near_three = gather_x(part_three.astype(bf16))
            twos = swap_all(to_all(factor_two.astype(bf16), n_row), "row")
            twos, near, near_y, near_three = lax.optimization_barrier((twos, near, near_y, near_three))
            ones = (near, near_y, swap(near, CORE), swap(near_y, CORE))
            threes = (near_three, swap(near_three, CORE))
    spread = learn_rate * ITERS
    new_three = place_third(ids, near, swap(near, CORE)).reshape(tile_depth, rank)
    return ((start_one - factor_one) / spread, (start_two - factor_two) / spread, new_three)


def solution(mesh):
    in_specs = (
        P("row", None, "col"),
        P("row", None, "col"),
        P(("row", "col"), None),
        P(("col", "row"), None),
        P(),
        P(("row", "col"), None),
        P(("row", "col"), None),
        P(("col", "row"), None),
        P(("col", "row"), None),
        P(),
        P(),
    )
    out_specs = (P(("row", "col"), None), P(("col", "row"), None), P())
    return jax.shard_map(shards, mesh=mesh, in_specs=in_specs, out_specs=out_specs, check_vma=False)
```

```python
import functools
import math

import jax
import jax.numpy as jnp
from jax import lax
from jax.experimental import pallas as pl
from jax.experimental.pallas import tpu as pltpu
from jax.sharding import PartitionSpec as P

ITERS = 2
STEP = 10
BLOCK = 64
SUB = 4
VMEM_LIMIT = 50 << 20
VMEM_ALL = 61 << 20
VMEM_LATER = 49 << 20

learn_rate = 0.05
beta_one = 0.8
beta_two = 0.95
adam_eps = 1e-08

f32 = jnp.float32
bf16 = jnp.bfloat16

CORE, Y_HI, X_ONE = 1, 2, 4


def adam_step(param, first, second, grad, counter):
    first = beta_one * first + (1.0 - beta_one) * grad
    second = beta_two * second + (1.0 - beta_two) * grad * grad
    corr_one = 1.0 - beta_one**counter
    corr_two = 1.0 - beta_two**counter
    param = param - learn_rate * (first / corr_one) / (jnp.sqrt(second / corr_two) + adam_eps)
    return (param, first, second)


def third_slab(col):
    return col // X_ONE * 2 + col % 2


def slope_kernel(scales, stepped, kind_hbm, data_ref, two_ref, near_ref, near_y_ref, far_ref, far_y_ref, *refs):
    if stepped:
        near_three_ref, far_three_ref, *refs = refs
    else:
        three_hbm, *refs = refs
    sent_ref, kept_ref, slope_ref, one_ref, three_ref, ga_acc, gc_acc, kind_ref, kind_sem, three_sem = refs
    step = pl.program_id(0)
    n_slab, own, rank = one_ref.shape
    depth = three_ref.shape[0] * three_ref.shape[1]
    cols = two_ref.shape[0] * two_ref.shape[1]
    here = lax.axis_index("col")

    @pl.when(step == 0)
    def _():
        kind_copy = pltpu.make_async_copy(kind_hbm.at[0, pl.ds(0, 8)], kind_ref, kind_sem)
        kind_copy.start()
        if not stepped:
            three_copy = pltpu.make_async_copy(three_hbm, gc_acc, three_sem)
            three_copy.start()
        for m in range(4):
            col = here ^ (m * X_ONE)
            one_ref[col] = near_ref[m]
            one_ref[col ^ Y_HI] = near_y_ref[m]
            one_ref[col ^ CORE] = far_ref[m]
            one_ref[col ^ CORE ^ Y_HI] = far_y_ref[m]
            if stepped:
                three_ref[third_slab(col)] = near_three_ref[m]
                three_ref[third_slab(col ^ CORE)] = far_three_ref[m]
        kind_copy.wait()
        if not stepped:
            three_copy.wait()
            three_ref[...] = gc_acc[...].astype(bf16)
        gc_acc[...] = jnp.zeros_like(gc_acc)

    def run(logistic):
        two = two_ref[...].reshape(cols, rank)
        three = three_ref[...].reshape(depth, rank)
        three_f = three.astype(f32)
        slabs = BLOCK // own
        one = one_ref[pl.ds(step * slabs, slabs)].reshape(BLOCK, rank)
        n = BLOCK // SUB

        def rows(s):
            return slice(s * SUB, (s + 1) * SUB)

        def rebuild(s):
            scaled = (one[rows(s)][:, None, :] * three[None]).reshape(SUB * depth, rank)
            return lax.dot_general(scaled, two, (((1,), (1,)), ((), ())), preferred_element_type=f32)

        def slope(s, rebuilt):
            values = data_ref[rows(s)].reshape(SUB * depth, cols).astype(f32)
            if logistic:
                out = 0.5 * jnp.tanh(0.5 * rebuilt) + jnp.where(values > 0, -0.5, 0.5)
            else:
                out = jnp.clip(rebuilt - values, -1.0, 1.0)
            out = out.astype(bf16)
            slope_ref[rows(s)] = out.reshape(SUB, depth, cols)
            return out

        def project(deriv):
            return jnp.dot(deriv, two, preferred_element_type=f32).reshape(SUB, depth, rank)

        rebuilt, derivs, projs = {}, {}, {}
        grad_one, grad_three = [], None
        for t in range(n + 3):
            if t < n:
                rebuilt[t] = rebuild(t)
            if 0 <= t - 1 < n:
                derivs[t - 1] = slope(t - 1, rebuilt.pop(t - 1))
            if 0 <= t - 2 < n:
                projs[t - 2] = project(derivs.pop(t - 2))
            if 0 <= t - 3 < n:
                proj = projs.pop(t - 3)
                one_f = one[rows(t - 3)].astype(f32)
                grad_one.append(jnp.sum(proj * three_f[None], axis=1))
                part = jnp.sum(proj * one_f[:, None, :], axis=0)
                grad_three = part if grad_three is None else grad_three + part
        ga_acc[pl.ds(step * slabs, slabs)] = jnp.concatenate(grad_one).reshape(slabs, own, rank)
        gc_acc[...] += grad_three.reshape(gc_acc.shape)

    pl.when(kind_ref[0, 0] == 1)(lambda: run(True))
    pl.when(kind_ref[0, 0] != 1)(lambda: run(False))

    @pl.when(step == pl.num_programs(0) - 1)
    def _():
        for side, out_ref in ((here, kept_ref), (here ^ CORE, sent_ref)):
            for m in range(4):
                col = side ^ (m * X_ONE)
                out_ref[m] = (ga_acc[col] * scales[0]).astype(bf16)
                out_ref[4 + m] = (gc_acc[third_slab(col)] * scales[2]).astype(bf16)
                out_ref[8 + m] = (ga_acc[col ^ Y_HI] * scales[0]).astype(bf16)


def slopes(loss_kind, tensor, twos, ones, threes, scales):
    rows, depth, cols = tensor.shape
    own, rank = ones[0].shape[1:]
    slabs = rows // own
    stepped = len(threes) == 2
    all_threes = (depth // threes[0].shape[1],) + threes[0].shape[1:]
    whole = lambda shape: pl.BlockSpec(shape, lambda i: (0,) * len(shape))
    swapped = (12, own, rank)
    return pl.pallas_call(
        functools.partial(slope_kernel, scales, stepped),
        grid=(rows // BLOCK,),
        in_specs=[
            pl.BlockSpec(memory_space=pltpu.HBM),
            pl.BlockSpec((BLOCK, depth, cols), lambda i: (i, 0, 0)),
            *[whole(x.shape) for x in (twos, *ones)],
            *([whole(x.shape) for x in threes] if stepped else [pl.BlockSpec(memory_space=pltpu.HBM)]),
        ],
        out_specs=[
            whole(swapped),
            whole(swapped),
            pl.BlockSpec((BLOCK, depth, cols), lambda i: (i, 0, 0)),
            whole((slabs, own, rank)),
            whole(all_threes),
        ],
        out_shape=[
            jax.ShapeDtypeStruct(swapped, bf16),
            jax.ShapeDtypeStruct(swapped, bf16),
            jax.ShapeDtypeStruct((rows, depth, cols), bf16),
            jax.ShapeDtypeStruct((slabs, own, rank), bf16),
            jax.ShapeDtypeStruct(all_threes, bf16),
        ],
        scratch_shapes=[
            pltpu.VMEM((slabs, own, rank), f32),
            pltpu.VMEM(all_threes, f32),
            pltpu.SMEM((8, cols), jnp.int32),
            pltpu.SemaphoreType.DMA,
            pltpu.SemaphoreType.DMA,
        ],
        compiler_params=pltpu.CompilerParams(vmem_limit_bytes=VMEM_LATER if stepped else VMEM_LIMIT),
        cost_estimate=pl.CostEstimate(
            flops=8 * rows * depth * cols * rank, bytes_accessed=4 << 20, transcendentals=rows * depth * cols
        ),
    )(loss_kind, tensor, twos, *ones, *threes)


def second_kernel(scale, slope_ref, one_ref, three_ref, out_ref, acc):
    step = pl.program_id(0)
    block, depth, cols = slope_ref.shape
    rank = one_ref.shape[2]
    one = one_ref[...].reshape(block, rank)
    three = three_ref[...].reshape(depth, rank)
    scaled = (one[:, None, :] * three[None]).reshape(block * depth, rank)
    part = lax.dot_general(
        slope_ref[...].reshape(block * depth, cols), scaled, (((0,), (0,)), ((), ())), preferred_element_type=f32
    )

    @pl.when(step == 0)
    def _():
        acc[...] = part

    @pl.when(step != 0)
    def _():
        acc[...] += part

    @pl.when(step == pl.num_programs(0) - 1)
    def _():
        out_ref[...] = (acc[...] * scale).astype(bf16)


def second_grad(slope, ones, threes, scale):
    rows, depth, cols = slope.shape
    slabs, own, rank = ones.shape
    block = 32
    return pl.pallas_call(
        functools.partial(second_kernel, scale),
        grid=(rows // block,),
        in_specs=[
            pl.BlockSpec((block, depth, cols), lambda i: (i, 0, 0)),
            pl.BlockSpec((block // own, own, rank), lambda i: (i, 0, 0)),
            pl.BlockSpec(threes.shape, lambda i: (0, 0, 0)),
        ],
        out_specs=pl.BlockSpec((cols, rank), lambda i: (0, 0)),
        out_shape=jax.ShapeDtypeStruct((cols, rank), bf16),
        scratch_shapes=[pltpu.VMEM((cols, rank), f32)],
        compiler_params=pltpu.CompilerParams(vmem_limit_bytes=VMEM_LIMIT),
        cost_estimate=pl.CostEstimate(
            flops=4 * rows * depth * cols * rank, bytes_accessed=2 << 20, transcendentals=0
        ),
    )(slope, ones, threes)


def copies_kernel(part_ref, out_ref):
    part = part_ref[...].astype(bf16)
    for slab in range(out_ref.shape[0]):
        out_ref[slab] = part


def copies(part, size):
    whole = lambda shape: pl.BlockSpec(shape, lambda i: (0,) * len(shape))
    out = (size,) + part.shape
    return pl.pallas_call(
        copies_kernel,
        grid=(1,),
        in_specs=[whole(part.shape)],
        out_specs=whole(out),
        out_shape=jax.ShapeDtypeStruct(out, bf16),
        compiler_params=pltpu.CompilerParams(vmem_limit_bytes=VMEM_ALL),
    )(part)


def place_kernel(near_ref, far_ref, out_ref):
    for m in range(4):
        col = lax.axis_index("col") ^ (m * X_ONE)
        out_ref[third_slab(col)] = near_ref[m]
        out_ref[third_slab(col ^ CORE)] = far_ref[m]


def place_third(near, far):
    slabs, own, rank = near.shape
    return pl.pallas_call(
        place_kernel,
        in_specs=[pl.BlockSpec(memory_space=pltpu.VMEM)] * 2,
        out_specs=pl.BlockSpec(memory_space=pltpu.VMEM),
        out_shape=jax.ShapeDtypeStruct((2 * slabs, own, rank), near.dtype),
        compiler_params=pltpu.CompilerParams(vmem_limit_bytes=8 << 20),
    )(near, far)


def update_kernel(counter, got_ref, *refs):
    two_in, three_in, two_out, three_out = refs[:3], refs[3:6], refs[6:9], refs[9:12]
    twos_ref, half_ref = refs[12:]
    own = two_in[0].shape[0]
    got = jnp.sum(got_ref[...].astype(f32), axis=0)
    for grad, old, new in ((got[:own], two_in, two_out), (got[own:], three_in, three_out)):
        for ref, value in zip(new, adam_step(*[x[...] for x in old], grad, counter)):
            ref[...] = value
    two = two_out[0][...].astype(bf16)
    for slab in range(twos_ref.shape[0]):
        twos_ref[slab] = two
    half_ref[...] = three_out[0][...].astype(bf16)


def update(got, two, three, counter):
    shapes = [jax.ShapeDtypeStruct(x.shape, f32) for x in (*two, *three)]
    twos = jax.ShapeDtypeStruct((got.shape[0],) + two[0].shape, bf16)
    vmem = pl.BlockSpec(memory_space=pltpu.VMEM)
    out = pl.pallas_call(
        functools.partial(update_kernel, counter),
        in_specs=[vmem] * 7,
        out_specs=[vmem] * 8,
        out_shape=[*shapes, twos, jax.ShapeDtypeStruct(three[0].shape, bf16)],
        compiler_params=pltpu.CompilerParams(vmem_limit_bytes=8 << 20),
    )(got, *two, *three)
    return out[:3], out[3:6], out[6], out[7]


def swap_all(parts, axis):
    return lax.all_to_all(parts, axis, 0, 0)


def to_all(part, size):
    return jnp.broadcast_to(part[None], (size,) + part.shape)


def total(parts):
    return jnp.sum(parts.astype(f32), axis=0)


def swap(part, code):
    size = lax.axis_size("col")
    return lax.ppermute(part, "col", [(i, i ^ code) for i in range(size)])


def plus(left, right):
    return (left.astype(f32) + right.astype(f32)).astype(bf16)


def gather_x(part):
    return jnp.stack([part] + [swap(part, m * X_ONE) for m in (1, 2, 3)])


def fold_kernel(both_ref, got_ref, out_ref):
    half = got_ref.shape[0] // 2
    for m in range(half):
        out_ref[m, 0] = plus(both_ref[m], got_ref[half + m])
        out_ref[m, 1] = plus(both_ref[half + m], got_ref[m])


def fold(both, got):
    slabs, own, rank = got.shape
    return pl.pallas_call(
        fold_kernel,
        in_specs=[pl.BlockSpec(memory_space=pltpu.VMEM)] * 2,
        out_specs=pl.BlockSpec(memory_space=pltpu.VMEM),
        out_shape=jax.ShapeDtypeStruct((slabs // 2, 2, own, rank), bf16),
        compiler_params=pltpu.CompilerParams(vmem_limit_bytes=8 << 20),
        cost_estimate=pl.CostEstimate(flops=1 << 16, bytes_accessed=1 << 18, transcendentals=0),
    )(both, got)


def reduce_col(both):
    pairs = fold(both, swap(both[4:], Y_HI))
    got = [swap(pairs[m], m * X_ONE) for m in (1, 2, 3)]
    out = pairs[0].astype(f32)
    for part in got:
        out = out + part.astype(f32)
    return out[0], out[1]


def shards(
    tensor, loss_kind, factor_one, factor_two, factor_three,
    first_one, second_one, first_two, second_two, first_three, second_three,
):
    tile_rows, tile_depth, tile_cols = tensor.shape
    n_row, n_col = lax.axis_size("row"), lax.axis_size("col")
    rank = factor_one.shape[1]
    own_two = factor_two.shape[0]
    deep = 2 * tile_depth // n_col
    full_rows, full_cols = tile_rows * n_row, tile_cols * n_col
    scales = (
        1.0 / math.sqrt(full_cols * tile_depth),
        1.0 / math.sqrt(full_rows * tile_depth),
        1.0 / math.sqrt(full_rows * full_cols),
    )
    here = lax.axis_index("col")
    mine = lambda x: lax.dynamic_slice_in_dim(x, third_slab(here) * deep, deep, 0)
    part_three, first_three, second_three = mine(factor_three), mine(first_three), mine(second_three)
    start_one, start_two, start_three = (factor_one, factor_two, part_three)
    twos = swap_all(copies(factor_two, n_row), "row")
    near = gather_x(factor_one.astype(bf16))
    near_y = swap(near, Y_HI)
    ones = (near, near_y, swap(near, CORE), swap(near_y, CORE))
    threes = (factor_three.reshape(tile_depth // deep, deep, rank),)
    for iteration in range(ITERS):
        last = iteration == ITERS - 1
        counter = STEP + iteration + 1
        sent, kept, slope, all_ones, all_threes = slopes(loss_kind, tensor, twos, ones, threes, scales)
        grad_two = second_grad(slope, all_ones, all_threes, scales[1]).reshape(n_row, own_two, rank)
        grad_one, grad_three = reduce_col(plus(kept, swap(sent, CORE)))
        sent = jnp.concatenate([grad_two, to_all(grad_three.astype(bf16), n_row)], axis=1)
        factor_one, first_one, second_one = adam_step(factor_one, first_one, second_one, grad_one, counter)
        got = swap_all(sent, "row")
        if last:
            got = total(got)
            grad_two, grad_three = got[:own_two], got[own_two:]
            part_three, first_three, second_three = adam_step(
                part_three, first_three, second_three, grad_three, counter
            )
            near_three = gather_x((start_three - part_three) / (learn_rate * ITERS))
            near_three, grad_two = lax.optimization_barrier((near_three, grad_two))
            factor_two, first_two, second_two = adam_step(
                factor_two, first_two, second_two, grad_two, counter
            )
        else:
            near = gather_x(factor_one.astype(bf16))
            got, near = lax.optimization_barrier((got, near))
            near_y = swap(near, Y_HI)
            two, three, sent, half_three = update(
                got, (factor_two, first_two, second_two), (part_three, first_three, second_three), counter
            )
            factor_two, first_two, second_two = two
            part_three, first_three, second_three = three
            near_three = gather_x(half_three)
            twos = swap_all(sent, "row")
            far = swap(jnp.concatenate([near, near_y, near_three]), CORE)
            ones = (near, near_y, far[:4], far[4:8])
            threes = (near_three, far[8:])
    spread = learn_rate * ITERS
    new_three = place_third(near_three, swap(near_three, CORE)).reshape(tile_depth, rank)
    return ((start_one - factor_one) / spread, (start_two - factor_two) / spread, new_three)


def solution(mesh):
    in_specs = (
        P("row", None, "col"),
        P("row", None, "col"),
        P(("row", "col"), None),
        P(("col", "row"), None),
        P(),
        P(("row", "col"), None),
        P(("row", "col"), None),
        P(("col", "row"), None),
        P(("col", "row"), None),
        P(),
        P(),
    )
    out_specs = (P(("row", "col"), None), P(("col", "row"), None), P())
    return jax.shard_map(shards, mesh=mesh, in_specs=in_specs, out_specs=out_specs, check_vma=False)
```

```python
import functools
import math

import jax
import jax.numpy as jnp
from jax import lax
from jax.experimental import pallas as pl
from jax.experimental.pallas import tpu as pltpu
from jax.sharding import PartitionSpec as P

ITERS = 2
STEP = 10
BLOCK = 64
SUB = 4
VMEM_LIMIT = 50 << 20
VMEM_ALL = 61 << 20
VMEM_LATER = 49 << 20

learn_rate = 0.05
beta_one = 0.8
beta_two = 0.95
adam_eps = 1e-08

f32 = jnp.float32
bf16 = jnp.bfloat16

CORE, Y_HI, X_ONE = 1, 2, 4


def adam_step(param, first, second, grad, counter):
    first = beta_one * first + (1.0 - beta_one) * grad
    second = beta_two * second + (1.0 - beta_two) * grad * grad
    corr_one = 1.0 - beta_one**counter
    corr_two = 1.0 - beta_two**counter
    param = param - learn_rate * (first / corr_one) / (jnp.sqrt(second / corr_two) + adam_eps)
    return (param, first, second)


def third_slab(col):
    return col // X_ONE * 2 + col % 2


def slope_kernel(scales, stepped, kind_ref, data_ref, two_ref, near_ref, near_y_ref, far_ref, far_y_ref, *refs):
    if stepped:
        near_three_ref, far_three_ref, *refs = refs
    else:
        three_in_ref, *refs = refs
    sent_ref, kept_ref, slope_ref, one_ref, three_ref, ga_acc, gc_acc = refs
    step = pl.program_id(0)
    n_slab, own, rank = one_ref.shape
    depth = three_ref.shape[0] * three_ref.shape[1]
    cols = two_ref.shape[0] * two_ref.shape[1]
    here = lax.axis_index("col")

    @pl.when(step == 0)
    def _():
        for m in range(4):
            col = here ^ (m * X_ONE)
            one_ref[col] = near_ref[m]
            one_ref[col ^ Y_HI] = near_y_ref[m]
            one_ref[col ^ CORE] = far_ref[m]
            one_ref[col ^ CORE ^ Y_HI] = far_y_ref[m]
            if stepped:
                three_ref[third_slab(col)] = near_three_ref[m]
                three_ref[third_slab(col ^ CORE)] = far_three_ref[m]
        if not stepped:
            three_ref[...] = three_in_ref[...].astype(bf16)
        gc_acc[...] = jnp.zeros_like(gc_acc)

    def run(logistic):
        two = two_ref[...].reshape(cols, rank)
        three = three_ref[...].reshape(depth, rank)
        three_f = three.astype(f32)
        slabs = BLOCK // own
        one = one_ref[pl.ds(step * slabs, slabs)].reshape(BLOCK, rank)
        n = BLOCK // SUB

        def rows(s):
            return slice(s * SUB, (s + 1) * SUB)

        def rebuild(s):
            scaled = (one[rows(s)][:, None, :] * three[None]).reshape(SUB * depth, rank)
            return lax.dot_general(scaled, two, (((1,), (1,)), ((), ())), preferred_element_type=f32)

        def slope(s, rebuilt):
            values = data_ref[rows(s)].reshape(SUB * depth, cols).astype(f32)
            if logistic:
                out = 0.5 * jnp.tanh(0.5 * rebuilt) + jnp.where(values > 0, -0.5, 0.5)
            else:
                out = jnp.clip(rebuilt - values, -1.0, 1.0)
            out = out.astype(bf16)
            slope_ref[rows(s)] = out.reshape(SUB, depth, cols)
            return out

        def project(deriv):
            return jnp.dot(deriv, two, preferred_element_type=f32).reshape(SUB, depth, rank)

        rebuilt, derivs, projs = {}, {}, {}
        grad_one, grad_three = [], None
        for t in range(n + 3):
            if t < n:
                rebuilt[t] = rebuild(t)
            if 0 <= t - 1 < n:
                derivs[t - 1] = slope(t - 1, rebuilt.pop(t - 1))
            if 0 <= t - 2 < n:
                projs[t - 2] = project(derivs.pop(t - 2))
            if 0 <= t - 3 < n:
                proj = projs.pop(t - 3)
                one_f = one[rows(t - 3)].astype(f32)
                grad_one.append(jnp.sum(proj * three_f[None], axis=1))
                part = jnp.sum(proj * one_f[:, None, :], axis=0)
                grad_three = part if grad_three is None else grad_three + part
        ga_acc[pl.ds(step * slabs, slabs)] = jnp.concatenate(grad_one).reshape(slabs, own, rank)
        gc_acc[...] += grad_three.reshape(gc_acc.shape)

    pl.when(kind_ref[0] == 1)(lambda: run(True))
    pl.when(kind_ref[0] != 1)(lambda: run(False))

    @pl.when(step == pl.num_programs(0) - 1)
    def _():
        for side, out_ref in ((here, kept_ref), (here ^ CORE, sent_ref)):
            for m in range(4):
                col = side ^ (m * X_ONE)
                out_ref[m] = (ga_acc[col] * scales[0]).astype(bf16)
                out_ref[4 + m] = (gc_acc[third_slab(col)] * scales[2]).astype(bf16)
                out_ref[8 + m] = (ga_acc[col ^ Y_HI] * scales[0]).astype(bf16)


def slopes(kind, tensor, twos, ones, threes, scales):
    rows, depth, cols = tensor.shape
    own, rank = ones[0].shape[1:]
    slabs = rows // own
    stepped = len(threes) == 2
    all_threes = (depth // threes[0].shape[1],) + threes[0].shape[1:]
    whole = lambda shape: pl.BlockSpec(shape, lambda i: (0,) * len(shape))
    swapped = (12, own, rank)
    return pl.pallas_call(
        functools.partial(slope_kernel, scales, stepped),
        grid=(rows // BLOCK,),
        in_specs=[
            pl.BlockSpec(memory_space=pltpu.SMEM),
            pl.BlockSpec((BLOCK, depth, cols), lambda i: (i, 0, 0)),
            *[whole(x.shape) for x in (twos, *ones, *threes)],
        ],
        out_specs=[
            whole(swapped),
            whole(swapped),
            pl.BlockSpec((BLOCK, depth, cols), lambda i: (i, 0, 0)),
            whole((slabs, own, rank)),
            whole(all_threes),
        ],
        out_shape=[
            jax.ShapeDtypeStruct(swapped, bf16),
            jax.ShapeDtypeStruct(swapped, bf16),
            jax.ShapeDtypeStruct((rows, depth, cols), bf16),
            jax.ShapeDtypeStruct((slabs, own, rank), bf16),
            jax.ShapeDtypeStruct(all_threes, bf16),
        ],
        scratch_shapes=[
            pltpu.VMEM((slabs, own, rank), f32),
            pltpu.VMEM(all_threes, f32),
        ],
        compiler_params=pltpu.CompilerParams(vmem_limit_bytes=VMEM_LATER if stepped else VMEM_LIMIT),
        cost_estimate=pl.CostEstimate(
            flops=8 * rows * depth * cols * rank, bytes_accessed=4 << 20, transcendentals=rows * depth * cols
        ),
    )(kind, tensor, twos, *ones, *threes)


def second_kernel(scale, slope_ref, one_ref, three_ref, out_ref, acc):
    step = pl.program_id(0)
    block, depth, cols = slope_ref.shape
    rank = one_ref.shape[2]
    one = one_ref[...].reshape(block, rank)
    three = three_ref[...].reshape(depth, rank)
    scaled = (one[:, None, :] * three[None]).reshape(block * depth, rank)
    part = lax.dot_general(
        slope_ref[...].reshape(block * depth, cols), scaled, (((0,), (0,)), ((), ())), preferred_element_type=f32
    )

    @pl.when(step == 0)
    def _():
        acc[...] = part

    @pl.when(step != 0)
    def _():
        acc[...] += part

    @pl.when(step == pl.num_programs(0) - 1)
    def _():
        out_ref[...] = (acc[...] * scale).astype(bf16)


def second_grad(slope, ones, threes, scale):
    rows, depth, cols = slope.shape
    slabs, own, rank = ones.shape
    block = 32
    return pl.pallas_call(
        functools.partial(second_kernel, scale),
        grid=(rows // block,),
        in_specs=[
            pl.BlockSpec((block, depth, cols), lambda i: (i, 0, 0)),
            pl.BlockSpec((block // own, own, rank), lambda i: (i, 0, 0)),
            pl.BlockSpec(threes.shape, lambda i: (0, 0, 0)),
        ],
        out_specs=pl.BlockSpec((cols, rank), lambda i: (0, 0)),
        out_shape=jax.ShapeDtypeStruct((cols, rank), bf16),
        scratch_shapes=[pltpu.VMEM((cols, rank), f32)],
        compiler_params=pltpu.CompilerParams(vmem_limit_bytes=VMEM_LIMIT),
        cost_estimate=pl.CostEstimate(
            flops=4 * rows * depth * cols * rank, bytes_accessed=2 << 20, transcendentals=0
        ),
    )(slope, ones, threes)


def copies_kernel(part_ref, out_ref):
    part = part_ref[...].astype(bf16)
    for slab in range(out_ref.shape[0]):
        out_ref[slab] = part


def copies(part, size):
    whole = lambda shape: pl.BlockSpec(shape, lambda i: (0,) * len(shape))
    out = (size,) + part.shape
    return pl.pallas_call(
        copies_kernel,
        grid=(1,),
        in_specs=[whole(part.shape)],
        out_specs=whole(out),
        out_shape=jax.ShapeDtypeStruct(out, bf16),
        compiler_params=pltpu.CompilerParams(vmem_limit_bytes=VMEM_ALL),
    )(part)


def place_kernel(near_ref, far_ref, out_ref):
    for m in range(4):
        col = lax.axis_index("col") ^ (m * X_ONE)
        out_ref[third_slab(col)] = near_ref[m]
        out_ref[third_slab(col ^ CORE)] = far_ref[m]


def place_third(near, far):
    slabs, own, rank = near.shape
    return pl.pallas_call(
        place_kernel,
        in_specs=[pl.BlockSpec(memory_space=pltpu.VMEM)] * 2,
        out_specs=pl.BlockSpec(memory_space=pltpu.VMEM),
        out_shape=jax.ShapeDtypeStruct((2 * slabs, own, rank), near.dtype),
        compiler_params=pltpu.CompilerParams(vmem_limit_bytes=8 << 20),
    )(near, far)


def update_kernel(counter, got_ref, *refs):
    two_in, three_in, two_out, three_out = refs[:3], refs[3:6], refs[6:9], refs[9:12]
    start_ref, twos_ref, half_ref = refs[12:]
    own = two_in[0].shape[0]
    slab = third_slab(lax.axis_index("col"))
    got = jnp.sum(got_ref[...].astype(f32), axis=0)
    two = adam_step(*[x[...] for x in two_in], got[:own], counter)
    three = adam_step(*[x[slab] for x in three_in], got[own:], counter)
    for ref, value in zip((*two_out, *three_out), (*two, *three)):
        ref[...] = value
    start_ref[...] = three_in[0][slab]
    half = two[0].astype(bf16)
    for place in range(twos_ref.shape[0]):
        twos_ref[place] = half
    half_ref[...] = three[0].astype(bf16)


def update(got, two, three, counter):
    rows = jax.ShapeDtypeStruct(two[0].shape, f32)
    third = jax.ShapeDtypeStruct(three[0].shape[1:], f32)
    twos = jax.ShapeDtypeStruct((got.shape[0],) + two[0].shape, bf16)
    vmem = pl.BlockSpec(memory_space=pltpu.VMEM)
    out = pl.pallas_call(
        functools.partial(update_kernel, counter),
        in_specs=[vmem] * 7,
        out_specs=[vmem] * 9,
        out_shape=[rows] * 3 + [third] * 4 + [twos, jax.ShapeDtypeStruct(third.shape, bf16)],
        compiler_params=pltpu.CompilerParams(vmem_limit_bytes=8 << 20),
    )(got, *two, *three)
    return out[:3], out[3:6], out[6], out[7], out[8]


def swap_all(parts, axis):
    return lax.all_to_all(parts, axis, 0, 0)


def to_all(part, size):
    return jnp.broadcast_to(part[None], (size,) + part.shape)


def total(parts):
    return jnp.sum(parts.astype(f32), axis=0)


def swap(part, code):
    size = lax.axis_size("col")
    return lax.ppermute(part, "col", [(i, i ^ code) for i in range(size)])


def plus(left, right):
    return (left.astype(f32) + right.astype(f32)).astype(bf16)


def gather_x(part):
    return jnp.stack([part] + [swap(part, m * X_ONE) for m in (1, 2, 3)])


def fold_kernel(both_ref, got_ref, out_ref):
    half = got_ref.shape[0] // 2
    for m in range(half):
        out_ref[m, 0] = plus(both_ref[m], got_ref[half + m])
        out_ref[m, 1] = plus(both_ref[half + m], got_ref[m])


def fold(both, got):
    slabs, own, rank = got.shape
    return pl.pallas_call(
        fold_kernel,
        in_specs=[pl.BlockSpec(memory_space=pltpu.VMEM)] * 2,
        out_specs=pl.BlockSpec(memory_space=pltpu.VMEM),
        out_shape=jax.ShapeDtypeStruct((slabs // 2, 2, own, rank), bf16),
        compiler_params=pltpu.CompilerParams(vmem_limit_bytes=8 << 20),
        cost_estimate=pl.CostEstimate(flops=1 << 16, bytes_accessed=1 << 18, transcendentals=0),
    )(both, got)


def reduce_col(both):
    pairs = fold(both, swap(both[4:], Y_HI))
    got = [swap(pairs[m], m * X_ONE) for m in (1, 2, 3)]
    out = pairs[0].astype(f32)
    for part in got:
        out = out + part.astype(f32)
    return out[0], out[1]


def shards(
    tensor, loss_kind, factor_one, factor_two, factor_three,
    first_one, second_one, first_two, second_two, first_three, second_three,
):
    tile_rows, tile_depth, tile_cols = tensor.shape
    n_row, n_col = lax.axis_size("row"), lax.axis_size("col")
    rank = factor_one.shape[1]
    own_two = factor_two.shape[0]
    deep = 2 * tile_depth // n_col
    full_rows, full_cols = tile_rows * n_row, tile_cols * n_col
    scales = (
        1.0 / math.sqrt(full_cols * tile_depth),
        1.0 / math.sqrt(full_rows * tile_depth),
        1.0 / math.sqrt(full_rows * full_cols),
    )
    start_one, start_two = factor_one, factor_two
    slabs = lambda x: x.reshape(tile_depth // deep, deep, rank)
    twos = swap_all(copies(factor_two, n_row), "row")
    near = gather_x(factor_one.astype(bf16))
    near_y = swap(near, Y_HI)
    ones = (near, near_y, swap(near, CORE), swap(near_y, CORE))
    threes = (slabs(factor_three),)
    kind = loss_kind[0, 0, :1]
    for iteration in range(ITERS):
        last = iteration == ITERS - 1
        counter = STEP + iteration + 1
        sent, kept, slope, all_ones, all_threes = slopes(kind, tensor, twos, ones, threes, scales)
        grad_two = second_grad(slope, all_ones, all_threes, scales[1]).reshape(n_row, own_two, rank)
        grad_one, grad_three = reduce_col(plus(kept, swap(sent, CORE)))
        sent = jnp.concatenate([grad_two, to_all(grad_three.astype(bf16), n_row)], axis=1)
        factor_one, first_one, second_one = adam_step(factor_one, first_one, second_one, grad_one, counter)
        got = swap_all(sent, "row")
        if last:
            got = total(got)
            grad_two, grad_three = got[:own_two], got[own_two:]
            part_three, first_three, second_three = adam_step(
                part_three, first_three, second_three, grad_three, counter
            )
            near_three = gather_x((start_three - part_three) / (learn_rate * ITERS))
            near_three, grad_two = lax.optimization_barrier((near_three, grad_two))
            factor_two, first_two, second_two = adam_step(
                factor_two, first_two, second_two, grad_two, counter
            )
        else:
            near = gather_x(factor_one.astype(bf16))
            got, near = lax.optimization_barrier((got, near))
            near_y = swap(near, Y_HI)
            third = [slabs(x) for x in (factor_three, first_three, second_three)]
            two, three, start_three, sent, half_three = update(
                got, (factor_two, first_two, second_two), third, counter
            )
            factor_two, first_two, second_two = two
            part_three, first_three, second_three = three
            near_three = gather_x(half_three)
            twos = swap_all(sent, "row")
            far = swap(jnp.concatenate([near, near_y, near_three]), CORE)
            ones = (near, near_y, far[:4], far[4:8])
            threes = (near_three, far[8:])
    spread = learn_rate * ITERS
    new_three = place_third(near_three, swap(near_three, CORE)).reshape(tile_depth, rank)
    return ((start_one - factor_one) / spread, (start_two - factor_two) / spread, new_three)


def solution(mesh):
    in_specs = (
        P("row", None, "col"),
        P("row", None, "col"),
        P(("row", "col"), None),
        P(("col", "row"), None),
        P(),
        P(("row", "col"), None),
        P(("row", "col"), None),
        P(("col", "row"), None),
        P(("col", "row"), None),
        P(),
        P(),
    )
    out_specs = (P(("row", "col"), None), P(("col", "row"), None), P())
    return jax.shard_map(shards, mesh=mesh, in_specs=in_specs, out_specs=out_specs, check_vma=False)
```

```python
import functools
import math

import jax
import jax.numpy as jnp
from jax import lax
from jax.experimental import pallas as pl
from jax.experimental.pallas import tpu as pltpu
from jax.sharding import PartitionSpec as P

ITERS = 2
STEP = 10
BLOCK = 64
SUB = 4
VMEM_LIMIT = 50 << 20
VMEM_ALL = 61 << 20
VMEM_LATER = 49 << 20

learn_rate = 0.05
beta_one = 0.8
beta_two = 0.95
adam_eps = 1e-08

f32 = jnp.float32
bf16 = jnp.bfloat16

CORE, Y_HI, X_ONE = 1, 2, 4


def adam_step(param, first, second, grad, counter):
    first = beta_one * first + (1.0 - beta_one) * grad
    second = beta_two * second + (1.0 - beta_two) * grad * grad
    corr_one = 1.0 - beta_one**counter
    corr_two = 1.0 - beta_two**counter
    param = param - learn_rate * (first / corr_one) / (jnp.sqrt(second / corr_two) + adam_eps)
    return (param, first, second)


def third_slab(col):
    return col // X_ONE * 2 + col % 2


def slope_kernel(scales, stepped, kind_ref, data_ref, two_ref, near_ref, near_y_ref, far_ref, far_y_ref, *refs):
    if stepped:
        near_three_ref, far_three_ref, *refs = refs
    else:
        three_in_ref, *refs = refs
    sent_ref, kept_ref, slope_ref, one_ref, three_ref, ga_acc, gc_acc = refs
    step = pl.program_id(0)
    n_slab, own, rank = one_ref.shape
    depth = three_ref.shape[0] * three_ref.shape[1]
    cols = two_ref.shape[0] * two_ref.shape[1]
    here = lax.axis_index("col")

    @pl.when(step == 0)
    def _():
        for m in range(4):
            col = here ^ (m * X_ONE)
            one_ref[col] = near_ref[m]
            one_ref[col ^ Y_HI] = near_y_ref[m]
            one_ref[col ^ CORE] = far_ref[m]
            one_ref[col ^ CORE ^ Y_HI] = far_y_ref[m]
            if stepped:
                three_ref[third_slab(col)] = near_three_ref[m]
                three_ref[third_slab(col ^ CORE)] = far_three_ref[m]
        if not stepped:
            three_ref[...] = three_in_ref[...].astype(bf16)
        gc_acc[...] = jnp.zeros_like(gc_acc)

    def run(logistic):
        two = two_ref[...].reshape(cols, rank)
        three = three_ref[...].reshape(depth, rank)
        three_f = three.astype(f32)
        slabs = BLOCK // own
        one = one_ref[pl.ds(step * slabs, slabs)].reshape(BLOCK, rank)
        n = BLOCK // SUB

        def rows(s):
            return slice(s * SUB, (s + 1) * SUB)

        def rebuild(s):
            scaled = (one[rows(s)][:, None, :] * three[None]).reshape(SUB * depth, rank)
            return lax.dot_general(scaled, two, (((1,), (1,)), ((), ())), preferred_element_type=f32)

        def slope(s, rebuilt):
            values = data_ref[rows(s)].reshape(SUB * depth, cols).astype(f32)
            if logistic:
                out = 0.5 * jnp.tanh(0.5 * rebuilt) + jnp.where(values > 0, -0.5, 0.5)
            else:
                out = jnp.clip(rebuilt - values, -1.0, 1.0)
            out = out.astype(bf16)
            slope_ref[rows(s)] = out.reshape(SUB, depth, cols)
            return out

        def project(deriv):
            return jnp.dot(deriv, two, preferred_element_type=f32).reshape(SUB, depth, rank)

        rebuilt, derivs, projs = {}, {}, {}
        grad_one, grad_three = [], None
        for t in range(n + 3):
            if t < n:
                rebuilt[t] = rebuild(t)
            if 0 <= t - 1 < n:
                derivs[t - 1] = slope(t - 1, rebuilt.pop(t - 1))
            if 0 <= t - 2 < n:
                projs[t - 2] = project(derivs.pop(t - 2))
            if 0 <= t - 3 < n:
                proj = projs.pop(t - 3)
                one_f = one[rows(t - 3)].astype(f32)
                grad_one.append(jnp.sum(proj * three_f[None], axis=1))
                part = jnp.sum(proj * one_f[:, None, :], axis=0)
                grad_three = part if grad_three is None else grad_three + part
        ga_acc[pl.ds(step * slabs, slabs)] = jnp.concatenate(grad_one).reshape(slabs, own, rank)
        gc_acc[...] += grad_three.reshape(gc_acc.shape)

    pl.when(kind_ref[0] % 2 == 1)(lambda: run(True))
    pl.when(kind_ref[0] % 2 != 1)(lambda: run(False))

    @pl.when(step == pl.num_programs(0) - 1)
    def _():
        for side, out_ref in ((here, kept_ref), (here ^ CORE, sent_ref)):
            for m in range(4):
                col = side ^ (m * X_ONE)
                out_ref[m] = (ga_acc[col] * scales[0]).astype(bf16)
                out_ref[4 + m] = (gc_acc[third_slab(col)] * scales[2]).astype(bf16)
                out_ref[8 + m] = (ga_acc[col ^ Y_HI] * scales[0]).astype(bf16)


def slopes(kind, tensor, twos, ones, threes, scales):
    rows, depth, cols = tensor.shape
    own, rank = ones[0].shape[1:]
    slabs = rows // own
    stepped = len(threes) == 2
    all_threes = (depth // threes[0].shape[1],) + threes[0].shape[1:]
    whole = lambda shape: pl.BlockSpec(shape, lambda i: (0,) * len(shape))
    swapped = (12, own, rank)
    return pl.pallas_call(
        functools.partial(slope_kernel, scales, stepped),
        grid=(rows // BLOCK,),
        in_specs=[
            pl.BlockSpec(memory_space=pltpu.SMEM),
            pl.BlockSpec((BLOCK, depth, cols), lambda i: (i, 0, 0)),
            *[whole(x.shape) for x in (twos, *ones, *threes)],
        ],
        out_specs=[
            whole(swapped),
            whole(swapped),
            pl.BlockSpec((BLOCK, depth, cols), lambda i: (i, 0, 0)),
            whole((slabs, own, rank)),
            whole(all_threes),
        ],
        out_shape=[
            jax.ShapeDtypeStruct(swapped, bf16),
            jax.ShapeDtypeStruct(swapped, bf16),
            jax.ShapeDtypeStruct((rows, depth, cols), bf16),
            jax.ShapeDtypeStruct((slabs, own, rank), bf16),
            jax.ShapeDtypeStruct(all_threes, bf16),
        ],
        scratch_shapes=[
            pltpu.VMEM((slabs, own, rank), f32),
            pltpu.VMEM(all_threes, f32),
        ],
        compiler_params=pltpu.CompilerParams(vmem_limit_bytes=VMEM_LATER if stepped else VMEM_LIMIT),
        cost_estimate=pl.CostEstimate(
            flops=8 * rows * depth * cols * rank, bytes_accessed=4 << 20, transcendentals=rows * depth * cols
        ),
    )(kind, tensor, twos, *ones, *threes)


def second_kernel(scale, slope_ref, one_ref, three_ref, out_ref, acc):
    step = pl.program_id(0)
    block, depth, cols = slope_ref.shape
    rank = one_ref.shape[2]
    one = one_ref[...].reshape(block, rank)
    three = three_ref[...].reshape(depth, rank)
    scaled = (one[:, None, :] * three[None]).reshape(block * depth, rank)
    part = lax.dot_general(
        slope_ref[...].reshape(block * depth, cols), scaled, (((0,), (0,)), ((), ())), preferred_element_type=f32
    )

    @pl.when(step == 0)
    def _():
        acc[...] = part

    @pl.when(step != 0)
    def _():
        acc[...] += part

    @pl.when(step == pl.num_programs(0) - 1)
    def _():
        out_ref[...] = (acc[...] * scale).astype(bf16)


def second_grad(slope, ones, threes, scale):
    rows, depth, cols = slope.shape
    slabs, own, rank = ones.shape
    block = 32
    return pl.pallas_call(
        functools.partial(second_kernel, scale),
        grid=(rows // block,),
        in_specs=[
            pl.BlockSpec((block, depth, cols), lambda i: (i, 0, 0)),
            pl.BlockSpec((block // own, own, rank), lambda i: (i, 0, 0)),
            pl.BlockSpec(threes.shape, lambda i: (0, 0, 0)),
        ],
        out_specs=pl.BlockSpec((cols, rank), lambda i: (0, 0)),
        out_shape=jax.ShapeDtypeStruct((cols, rank), bf16),
        scratch_shapes=[pltpu.VMEM((cols, rank), f32)],
        compiler_params=pltpu.CompilerParams(vmem_limit_bytes=VMEM_LIMIT),
        cost_estimate=pl.CostEstimate(
            flops=4 * rows * depth * cols * rank, bytes_accessed=2 << 20, transcendentals=0
        ),
    )(slope, ones, threes)


def copies_kernel(part_ref, out_ref):
    part = part_ref[...].astype(bf16)
    for slab in range(out_ref.shape[0]):
        out_ref[slab] = part


def copies(part, size):
    whole = lambda shape: pl.BlockSpec(shape, lambda i: (0,) * len(shape))
    out = (size,) + part.shape
    return pl.pallas_call(
        copies_kernel,
        grid=(1,),
        in_specs=[whole(part.shape)],
        out_specs=whole(out),
        out_shape=jax.ShapeDtypeStruct(out, bf16),
        compiler_params=pltpu.CompilerParams(vmem_limit_bytes=VMEM_ALL),
    )(part)


def place_kernel(near_ref, far_ref, out_ref):
    for m in range(4):
        col = lax.axis_index("col") ^ (m * X_ONE)
        out_ref[third_slab(col)] = near_ref[m]
        out_ref[third_slab(col ^ CORE)] = far_ref[m]


def place_third(near, far):
    slabs, own, rank = near.shape
    return pl.pallas_call(
        place_kernel,
        in_specs=[pl.BlockSpec(memory_space=pltpu.VMEM)] * 2,
        out_specs=pl.BlockSpec(memory_space=pltpu.VMEM),
        out_shape=jax.ShapeDtypeStruct((2 * slabs, own, rank), near.dtype),
        compiler_params=pltpu.CompilerParams(vmem_limit_bytes=8 << 20),
    )(near, far)


def update_kernel(counter, grad_ref, got_ref, *refs):
    one_in, two_in, three_in = refs[:3], refs[3:6], refs[6:9]
    new_refs = refs[9:18]
    start_ref, twos_ref, pair_ref = refs[18:]
    own = two_in[0].shape[0]
    slab = third_slab(lax.axis_index("col"))
    got = jnp.sum(got_ref[...].astype(f32), axis=0)
    one = adam_step(*[x[...] for x in one_in], grad_ref[0], counter)
    two = adam_step(*[x[...] for x in two_in], got[:own], counter)
    three = adam_step(*[x[slab] for x in three_in], got[own:], counter)
    for ref, value in zip(new_refs, (*one, *two, *three)):
        ref[...] = value
    start_ref[...] = three_in[0][slab]
    half = two[0].astype(bf16)
    for place in range(twos_ref.shape[0]):
        twos_ref[place] = half
    pair_ref[0] = one[0].astype(bf16)
    pair_ref[1] = three[0].astype(bf16)


def update(grads, got, one, two, three, counter):
    rows = jax.ShapeDtypeStruct(two[0].shape, f32)
    third = jax.ShapeDtypeStruct(three[0].shape[1:], f32)
    twos = jax.ShapeDtypeStruct((got.shape[0],) + two[0].shape, bf16)
    vmem = pl.BlockSpec(memory_space=pltpu.VMEM)
    out = pl.pallas_call(
        functools.partial(update_kernel, counter),
        in_specs=[vmem] * 11,
        out_specs=[vmem] * 12,
        out_shape=[rows] * 6 + [third] * 4 + [twos, jax.ShapeDtypeStruct((2,) + third.shape, bf16)],
        compiler_params=pltpu.CompilerParams(vmem_limit_bytes=8 << 20),
    )(grads, got, *one, *two, *three)
    return out[:3], out[3:6], out[6:9], out[9], out[10], out[11]


def swap_all(parts, axis):
    return lax.all_to_all(parts, axis, 0, 0)


def to_all(part, size):
    return jnp.broadcast_to(part[None], (size,) + part.shape)


def total(parts):
    return jnp.sum(parts.astype(f32), axis=0)


def swap(part, code):
    size = lax.axis_size("col")
    return lax.ppermute(part, "col", [(i, i ^ code) for i in range(size)])


def plus(left, right):
    return (left.astype(f32) + right.astype(f32)).astype(bf16)


def gather_x(part):
    return jnp.stack([part] + [swap(part, m * X_ONE) for m in (1, 2, 3)])


def fold_kernel(both_ref, got_ref, out_ref):
    half = got_ref.shape[0] // 2
    for m in range(half):
        out_ref[m, 0] = plus(both_ref[m], got_ref[half + m])
        out_ref[m, 1] = plus(both_ref[half + m], got_ref[m])


def fold(both, got):
    slabs, own, rank = got.shape
    return pl.pallas_call(
        fold_kernel,
        in_specs=[pl.BlockSpec(memory_space=pltpu.VMEM)] * 2,
        out_specs=pl.BlockSpec(memory_space=pltpu.VMEM),
        out_shape=jax.ShapeDtypeStruct((slabs // 2, 2, own, rank), bf16),
        compiler_params=pltpu.CompilerParams(vmem_limit_bytes=8 << 20),
        cost_estimate=pl.CostEstimate(flops=1 << 16, bytes_accessed=1 << 18, transcendentals=0),
    )(both, got)


def reduce_col(both):
    pairs = fold(both, swap(both[4:], Y_HI))
    got = [swap(pairs[m], m * X_ONE) for m in (1, 2, 3)]
    out = pairs[0].astype(f32)
    for part in got:
        out = out + part.astype(f32)
    return out


def shards(
    tensor, loss_kind, factor_one, factor_two, factor_three,
    first_one, second_one, first_two, second_two, first_three, second_three,
):
    tile_rows, tile_depth, tile_cols = tensor.shape
    n_row, n_col = lax.axis_size("row"), lax.axis_size("col")
    rank = factor_one.shape[1]
    own_two = factor_two.shape[0]
    deep = 2 * tile_depth // n_col
    full_rows, full_cols = tile_rows * n_row, tile_cols * n_col
    scales = (
        1.0 / math.sqrt(full_cols * tile_depth),
        1.0 / math.sqrt(full_rows * tile_depth),
        1.0 / math.sqrt(full_rows * full_cols),
    )
    start_one, start_two = factor_one, factor_two
    slabs = lambda x: x.reshape(tile_depth // deep, deep, rank)
    twos = swap_all(copies(factor_two, n_row), "row")
    near = gather_x(factor_one.astype(bf16))
    near_y = swap(near, Y_HI)
    ones = (near, near_y, swap(near, CORE), swap(near_y, CORE))
    threes = (slabs(factor_three),)
    kind = loss_kind[0, 0, :1] + 2 * lax.axis_index("col")
    for iteration in range(ITERS):
        last = iteration == ITERS - 1
        counter = STEP + iteration + 1
        sent, kept, slope, all_ones, all_threes = slopes(kind, tensor, twos, ones, threes, scales)
        grad_two = second_grad(slope, all_ones, all_threes, scales[1]).reshape(n_row, own_two, rank)
        grads = reduce_col(plus(kept, swap(sent, CORE)))
        sent = jnp.concatenate([grad_two, to_all(grads[1].astype(bf16), n_row)], axis=1)
        got = swap_all(sent, "row")
        if last:
            factor_one, first_one, second_one = adam_step(
                factor_one, first_one, second_one, grads[0], counter
            )
            got = total(got)
            grad_two, grad_three = got[:own_two], got[own_two:]
            part_three, first_three, second_three = adam_step(
                part_three, first_three, second_three, grad_three, counter
            )
            near_three = gather_x((start_three - part_three) / (learn_rate * ITERS))
            near_three, grad_two = lax.optimization_barrier((near_three, grad_two))
            factor_two, first_two, second_two = adam_step(
                factor_two, first_two, second_two, grad_two, counter
            )
        else:
            third = [slabs(x) for x in (factor_three, first_three, second_three)]
            one, two, three, start_three, sent, pair = update(
                grads, got, (factor_one, first_one, second_one), (factor_two, first_two, second_two), third, counter
            )
            factor_one, first_one, second_one = one
            factor_two, first_two, second_two = two
            part_three, first_three, second_three = three
            twos = swap_all(sent, "row")
            half = gather_x(pair)
            near, near_three = half[:, 0], half[:, 1]
            near_y = swap(near, Y_HI)
            ones = (near, near_y, swap(near, CORE), swap(near_y, CORE))
            threes = (near_three, swap(near_three, CORE))
    spread = learn_rate * ITERS
    new_three = place_third(near_three, swap(near_three, CORE)).reshape(tile_depth, rank)
    return ((start_one - factor_one) / spread, (start_two - factor_two) / spread, new_three)


def solution(mesh):
    in_specs = (
        P("row", None, "col"),
        P("row", None, "col"),
        P(("row", "col"), None),
        P(("col", "row"), None),
        P(),
        P(("row", "col"), None),
        P(("row", "col"), None),
        P(("col", "row"), None),
        P(("col", "row"), None),
        P(),
        P(),
    )
    out_specs = (P(("row", "col"), None), P(("col", "row"), None), P())
    return jax.shard_map(shards, mesh=mesh, in_specs=in_specs, out_specs=out_specs, check_vma=False)
```
